32 devices in a mesh: dp: 4 (over y, core), loop: 8 (over z, x).
Axes of the slice: x: 2, y: 2, z: 4, core: 2. Of those that a mesh axis runs over, the one named last changes fastest.
Arguments:
- image_embeds: bfloat16 [4096, 1152], P(('dp', 'loop')), may hold values from -0.6 to 0.6
- text_embeds: bfloat16 [4096, 1152], P(('dp', 'loop')), may hold values from -0.6 to 0.6
- log_scale: float32 [1], replicated, may hold values from 2 to 2.7
- logit_bias: float32 [1], replicated, may hold values from -8 to -5
Outputs:
- loss: float32 [1], replicated
- image_grad: bfloat16 [4096, 1152], P(('dp', 'loop'))
- text_grad: bfloat16 [4096, 1152], P(('dp', 'loop'))
- grad_log_scale: float32 [1], replicated
- grad_bias: float32 [1], replicated
The draws below stay inside these ranges and needn't reach their ends.
All inputs are finite; a program needn't handle non-finite values.
Results may differ from the reference program's by a relative error of at most 0.0065.
Values may be sent and summed in bfloat16 or wider, within the bound.
A program may use at most 64 MiB of HBM per device.

```python
import math
import jax
import jax.numpy as jnp
from jax import lax

D = 1152
ROWS_DEV = 128
GROUP = 512
BATCH = 4096
N_DP = 4
N_LOOP = 8


def shared_rows(key):
    key = jax.random.fold_in(key, 11)
    keys = jax.random.split(key, 3)
    clusters = max(GROUP // 8, 1)
    members = jax.random.randint(keys[0], (BATCH,), 0, clusters)
    centers = jnp.clip(jax.random.normal(keys[1], (clusters, D), jnp.float32), -4.0, 4.0)
    single = jnp.clip(jax.random.normal(keys[2], (BATCH, D), jnp.float32), -4.0, 4.0)
    return 0.5 * jnp.take(centers, members, axis=0) + 0.59 * single


def draw_image_embeds(key, part):
    base = shared_rows(key)
    key = jax.random.fold_in(key, 3)
    noise_key, scale_key = jax.random.split(key)
    noise = jnp.clip(jax.random.normal(noise_key, (BATCH, D), jnp.float32), -4.0, 4.0)
    scales = jnp.exp(jax.random.uniform(scale_key, (BATCH, 1), jnp.float32, math.log(0.02), math.log(0.05)))
    return (scales * (base + 0.63 * noise)).astype(jnp.bfloat16)


def draw_text_embeds(key, part):
    base = shared_rows(key)
    key = jax.random.fold_in(key, 5)
    noise_key, scale_key = jax.random.split(key)
    noise = jnp.clip(jax.random.normal(noise_key, (BATCH, D), jnp.float32), -4.0, 4.0)
    scales = jnp.exp(jax.random.uniform(scale_key, (BATCH, 1), jnp.float32, math.log(0.02), math.log(0.05)))
    return (scales * (base + 0.63 * noise)).astype(jnp.bfloat16)


def setup_inputs(seed: int = 0) -> dict:
    splits = jax.random.split(jax.random.key(seed), 5)
    return {
        "image_embeds": draw_image_embeds(jax.random.fold_in(splits[4], 71), 0),
        "text_embeds": draw_text_embeds(jax.random.fold_in(splits[4], 71), 0),
        "log_scale": jnp.clip(jax.random.uniform(splits[2], (1,), jnp.float32, 2.0, 2.7), 2.0, 2.7),
        "logit_bias": jnp.clip(jax.random.uniform(splits[3], (1,), jnp.float32, -8.0, -5.0), -8.0, -5.0),
    }


EPSILON = 1e-06

def unit_rows(matrix):
    floats = matrix.astype(jnp.float32)
    return floats * lax.rsqrt(lax.optimization_barrier(jnp.sum(floats * floats, axis=1, keepdims=True)) + EPSILON)

def unit_pull(matrix, cotangent):
    _, pullback = jax.vjp(unit_rows, matrix.astype(jnp.float32))
    return pullback(cotangent)[0]

def rounded(values):
    return lax.optimization_barrier(values.astype(jnp.bfloat16)).astype(jnp.float32)

def to_groups(matrix):
    return matrix.reshape(N_DP, N_LOOP, ROWS_DEV, D).transpose(1, 0, 2, 3).reshape(N_LOOP, N_DP * ROWS_DEV, D)

def from_groups(matrix):
    return matrix.reshape(N_LOOP, N_DP, ROWS_DEV, D).transpose(1, 0, 2, 3).reshape(BATCH, D)

def reference(image_embeds, text_embeds, log_scale, logit_bias):
    temper = jnp.exp(log_scale[0])
    offset = logit_bias[0]
    image_groups = to_groups(unit_rows(image_embeds).astype(jnp.bfloat16).astype(jnp.float32))
    text_groups = to_groups(unit_rows(text_embeds).astype(jnp.bfloat16).astype(jnp.float32))
    member_ids = jnp.arange(N_DP * ROWS_DEV, dtype=jnp.int32)
    positive = member_ids[:, None] == member_ids[None, :]
    signs = jnp.where(positive, jnp.float32(-1.0), jnp.float32(1.0))

    def group_step(carry, group):
        loss_acc, scale_acc, bias_acc = carry
        images_here = lax.dynamic_index_in_dim(image_groups, group, 0, keepdims=False)
        texts_here = lax.dynamic_index_in_dim(text_groups, group, 0, keepdims=False)
        scaled = temper * jnp.einsum('ad,cd->ac', images_here, texts_here)
        logits = scaled + offset
        losses = jax.nn.softplus(signs * logits)
        coef = jax.nn.sigmoid(logits) - positive.astype(jnp.float32)
        coef_half = rounded(coef)
        image_term = temper * jnp.einsum('ac,cd->ad', coef_half, texts_here)
        text_term = temper * jnp.einsum('ac,ad->cd', coef_half, images_here)
        new_carry = (loss_acc + jnp.sum(losses), scale_acc + jnp.sum(coef * scaled), bias_acc + jnp.sum(coef))
        return (new_carry, (image_term, text_term))
    start = (jnp.zeros((), jnp.float32), jnp.zeros((), jnp.float32), jnp.zeros((), jnp.float32))
    groups = jnp.arange(N_LOOP, dtype=jnp.int32)
    final, terms = lax.scan(group_step, start, groups)
    loss_acc, scale_acc, bias_acc = final
    image_cot = from_groups(terms[0])
    text_cot = from_groups(terms[1])
    image_grad = unit_pull(image_embeds, image_cot).astype(jnp.bfloat16)
    text_grad = unit_pull(text_embeds, text_cot).astype(jnp.bfloat16)
    loss = jnp.reshape(loss_acc / BATCH, (1,))
    return (loss, image_grad, text_grad, jnp.reshape(scale_acc, (1,)), jnp.reshape(bias_acc, (1,)))
```

```python
import functools

import jax
import jax.numpy as jnp
from jax import lax
from jax.experimental import pallas as pl
from jax.experimental.pallas import tpu as pltpu
from jax.sharding import PartitionSpec as P

EPSILON = 1e-06
TEXT, IMAGE = 0, 1
CHUNKS = (2, 4)


def inverse_norm(floats):
    return lax.rsqrt(jnp.sum(floats * floats, axis=1, keepdims=True) + EPSILON)


def softplus_and_sigmoid(logits):
    small = jnp.exp(-jnp.abs(logits))
    softplus = jnp.maximum(logits, 0.0) + jnp.log1p(small)
    sigmoid = jnp.where(logits >= 0.0, 1.0, small) / (1.0 + small)
    return softplus, sigmoid


def dot_nt(left, right):
    return lax.dot_general(
        left, right, (((1,), (1,)), ((), ())), preferred_element_type=jnp.float32
    )


def unit_pull(embeds, cot, temper):
    floats = embeds.astype(jnp.float32)
    r = inverse_norm(floats)
    along = jnp.sum(floats * cot, axis=1, keepdims=True)
    return ((temper * r) * (cot - floats * (r * r * along))).astype(jnp.bfloat16)


def kernel(
    n_dp, n_loop, inverse_batch,
    image_hbm, text_hbm, scale_ref, bias_ref,
    loss_ref, image_grad_hbm, text_grad_hbm, scale_grad_ref, bias_grad_ref,
    own, units, total, grads, dp_sums, loop_sums,
    load_sem, store_sem, send_sem, recv_sem, pass_sem, sum_send, sum_recv,
):
    rows = own.shape[1]
    chips = n_dp // 2
    dp, loop = lax.axis_index("dp"), lax.axis_index("loop")
    core = lax.rem(dp, 2)
    sibling = dp + 1 - 2 * core

    def peer_dp(step):
        return lax.rem(dp + step, n_dp)

    def peer_loop(step):
        return lax.rem(loop + step, n_loop)

    barrier = pltpu.get_barrier_semaphore()
    for step in range(1, n_dp):
        pl.semaphore_signal(barrier, inc=1, device_id={"dp": peer_dp(step)}, device_id_type=pl.DeviceIdType.MESH)
    for step in range(1, n_loop):
        pl.semaphore_signal(barrier, inc=1, device_id={"loop": peer_loop(step)}, device_id_type=pl.DeviceIdType.MESH)

    loads = []
    for kind, source in ((TEXT, text_hbm), (IMAGE, image_hbm)):
        loads.append(pltpu.make_async_copy(source, own.at[kind], load_sem.at[kind]))
        loads[-1].start()

    def normalize(kind):
        loads[kind].wait()
        floats = own[kind].astype(jnp.float32)
        units[kind, 0] = (floats * inverse_norm(floats)).astype(jnp.bfloat16)

    def piece(kind, part):
        size = rows // CHUNKS[kind]
        return pl.ds(part * size, size)

    def copy(kind, part, from_slot, to_slot, target, sem):
        return pltpu.make_async_remote_copy(
            src_ref=units.at[kind, from_slot, piece(kind, part)],
            dst_ref=units.at[kind, to_slot, piece(kind, part)],
            send_sem=sem.at[kind, to_slot, part],
            recv_sem=recv_sem.at[kind, to_slot, part],
            device_id={"dp": target},
            device_id_type=pl.DeviceIdType.MESH,
        )

    sent = []

    def send(kind):
        for part in range(CHUNKS[kind]):
            for k in range(1, chips):
                sent.append(copy(kind, part, 0, 2 * k, peer_dp(2 * k), send_sem))
                sent[-1].start()
        for part in range(CHUNKS[kind]):
            sent.append(copy(kind, part, 0, 1, sibling, send_sem))
            sent[-1].start()

    def arrival(kind, part, slot):
        return copy(kind, part, 0, slot, sibling, send_sem)

    def pass_on(kind, part):
        for k in range(1, chips):
            arrival(kind, part, 2 * k).wait_recv()
            sent.append(copy(kind, part, 2 * k, 2 * k + 1, sibling, pass_sem))
            sent[-1].start()

    normalize(TEXT)
    pl.semaphore_wait(barrier, n_dp + n_loop - 2)
    send(TEXT)
    normalize(IMAGE)
    send(IMAGE)

    temper_vec = jnp.exp(jnp.full((1, 128), scale_ref[0], jnp.float32))
    temper = temper_vec[:, :1]
    offset = bias_ref[0]
    image_unit = units[IMAGE, 0]
    text_unit = units[TEXT, 0]

    def eye():
        ids = lax.broadcasted_iota(jnp.int32, (rows, rows), 0)
        return ids == lax.broadcasted_iota(jnp.int32, (rows, rows), 1)

    sums = [jnp.zeros((rows, 128), jnp.float32) for _ in range(3)]

    def folded(values):
        return sum(values[:, c:c + 128] for c in range(0, values.shape[1], 128))

    def row_pair(k, first):
        texts = units[TEXT, 2 * k:2 * k + 2].reshape(2 * rows, -1)
        scaled = temper * dot_nt(image_unit, texts)
        logits = scaled + offset
        losses, coef = softplus_and_sigmoid(logits)
        if first:
            wide = jnp.concatenate([eye(), jnp.zeros((rows, rows), jnp.bool_)], axis=1)
            losses = jnp.where(wide, losses - logits, losses)
            coef = jnp.where(wide, coef - 1.0, coef)
        for i, values in enumerate((losses, coef * scaled, coef)):
            sums[i] += folded(values)
        return jnp.dot(coef.astype(jnp.bfloat16), texts, preferred_element_type=jnp.float32)

    def col_part(images, diagonal):
        logits = temper * dot_nt(text_unit, images) + offset
        _, coef = softplus_and_sigmoid(logits)
        if diagonal:
            coef = jnp.where(eye(), coef - 1.0, coef)
        return jnp.dot(coef.astype(jnp.bfloat16), images, preferred_element_type=jnp.float32)

    for part in range(CHUNKS[TEXT]):
        arrival(TEXT, part, 1).wait_recv()
    total[...] = row_pair(0, True)
    for part in range(CHUNKS[TEXT]):
        pass_on(TEXT, part)
    for k in range(1, chips):
        for part in range(CHUNKS[TEXT]):
            arrival(TEXT, part, 2 * k + 1).wait_recv()
        total[...] += row_pair(k, False)

    def exchange(stage, buffer, count, target, axis):
        copies = []
        for step in range(1, count):
            copies.append(pltpu.make_async_remote_copy(
                src_ref=buffer.at[0],
                dst_ref=buffer.at[step],
                send_sem=sum_send.at[stage, step],
                recv_sem=sum_recv.at[stage, step],
                device_id={axis: target(step)},
                device_id_type=pl.DeviceIdType.MESH,
            ))
            copies[-1].start()
        return copies

    dp_sums[0] = jnp.concatenate(
        [jnp.sum(s, axis=0, keepdims=True) for s in sums] + [jnp.zeros((5, 128), jnp.float32)], axis=0
    )
    dp_copies = exchange(0, dp_sums, n_dp, peer_dp, "dp")

    grads[IMAGE] = unit_pull(own[IMAGE], total[...], temper)
    image_store = pltpu.make_async_copy(grads.at[IMAGE], image_grad_hbm, store_sem.at[IMAGE])
    image_store.start()

    total[...] = col_part(image_unit, True)
    for part in range(CHUNKS[IMAGE]):
        arrival(IMAGE, part, 1).wait_recv()
    total[...] += col_part(units[IMAGE, 1], False)

    for c in dp_copies:
        c.wait_recv()
    loop_sums[0] = jnp.sum(dp_sums[...], axis=0)
    loop_copies = exchange(1, loop_sums, n_loop, peer_loop, "loop")

    for part in range(CHUNKS[IMAGE]):
        pass_on(IMAGE, part)
        for k in range(1, chips):
            total[...] += col_part(units[IMAGE, 2 * k, piece(IMAGE, part)], False)
            arrival(IMAGE, part, 2 * k + 1).wait_recv()
            total[...] += col_part(units[IMAGE, 2 * k + 1, piece(IMAGE, part)], False)
    grads[TEXT] = unit_pull(own[TEXT], total[...], temper)
    text_store = pltpu.make_async_copy(grads.at[TEXT], text_grad_hbm, store_sem.at[TEXT])
    text_store.start()

    for c in loop_copies:
        c.wait_recv()
    final = jnp.sum(loop_sums[...], axis=0)
    loss_ref[0] = jnp.sum(final[0:1, :]) * inverse_batch
    scale_grad_ref[0] = jnp.sum(final[1:2, :])
    bias_grad_ref[0] = jnp.sum(final[2:3, :])

    for c in sent + dp_copies + loop_copies:
        c.wait_send()
    image_store.wait()
    text_store.wait()


def solution(mesh):
    n_dp, n_loop = mesh.shape["dp"], mesh.shape["loop"]

    def on_device(image_embeds, text_embeds, log_scale, logit_bias):
        rows, width = image_embeds.shape
        scalar = jax.ShapeDtypeStruct((1,), jnp.float32)
        grad = jax.ShapeDtypeStruct((rows, width), jnp.bfloat16)
        anywhere = pl.BlockSpec(memory_space=pl.ANY)
        smem = pl.BlockSpec(memory_space=pltpu.SMEM)
        parts = max(CHUNKS)
        return pl.pallas_call(
            functools.partial(kernel, n_dp, n_loop, 1.0 / (rows * n_dp * n_loop)),
            out_shape=(scalar, grad, grad, scalar, scalar),
            in_specs=[anywhere, anywhere, smem, smem],
            out_specs=(smem, anywhere, anywhere, smem, smem),
            scratch_shapes=[
                pltpu.VMEM((2, rows, width), jnp.bfloat16),
                pltpu.VMEM((2, n_dp, rows, width), jnp.bfloat16),
                pltpu.VMEM((rows, width), jnp.float32),
                pltpu.VMEM((2, rows, width), jnp.bfloat16),
                pltpu.VMEM((n_dp, 8, 128), jnp.float32),
                pltpu.VMEM((n_loop, 8, 128), jnp.float32),
                pltpu.SemaphoreType.DMA((2,)),
                pltpu.SemaphoreType.DMA((2,)),
                pltpu.SemaphoreType.DMA((2, n_dp, parts)),
                pltpu.SemaphoreType.DMA((2, n_dp, parts)),
                pltpu.SemaphoreType.DMA((2, n_dp, parts)),
                pltpu.SemaphoreType.DMA((2, max(n_dp, n_loop))),
                pltpu.SemaphoreType.DMA((2, max(n_dp, n_loop))),
            ],
            compiler_params=pltpu.CompilerParams(
                collective_id=0, has_side_effects=True, vmem_limit_bytes=32 * 1024 * 1024
            ),
        )(image_embeds, text_embeds, log_scale, logit_bias)

    return jax.shard_map(
        on_device,
        mesh=mesh,
        in_specs=(P(("dp", "loop"), None), P(("dp", "loop"), None), P(), P()),
        out_specs=(P(), P(("dp", "loop"), None), P(("dp", "loop"), None), P(), P()),
        check_vma=False,
    )
```

```python
import functools

import jax
import jax.numpy as jnp
from jax import lax
from jax.experimental import pallas as pl
from jax.experimental.pallas import tpu as pltpu
from jax.sharding import PartitionSpec as P

EPSILON = 1e-06
TEXT, IMAGE = 0, 1
CHUNKS = (2, 2)


def inverse_norm(floats):
    return lax.rsqrt(jnp.sum(floats * floats, axis=1, keepdims=True) + EPSILON)


def softplus_and_sigmoid(logits):
    small = jnp.exp(-jnp.abs(logits))
    softplus = jnp.maximum(logits, 0.0) + jnp.log1p(small)
    sigmoid = jnp.where(logits >= 0.0, 1.0, small) / (1.0 + small)
    return softplus, sigmoid


def dot_nt(left, right):
    return lax.dot_general(
        left, right, (((1,), (1,)), ((), ())), preferred_element_type=jnp.float32
    )


def unit_pull(embeds, r, cot, temper):
    floats = embeds.astype(jnp.float32)
    along = jnp.sum(floats * cot, axis=1, keepdims=True)
    return ((temper * r) * (cot - floats * (r * r * along))).astype(jnp.bfloat16)


def kernel(
    n_dp, n_loop,
    image_hbm, text_hbm, scale_ref, bias_ref,
    image_grad_ref, text_grad_ref, sums_ref,
    own, units, total, norms, dp_sums, loop_sums,
    load_sem, send_sem, recv_sem, pass_sem, sum_send, sum_recv,
):
    rows = own.shape[1]
    chips = n_dp // 2
    dp, loop = lax.axis_index("dp"), lax.axis_index("loop")
    core = lax.rem(dp, 2)
    sibling = dp + 1 - 2 * core

    def peer_dp(step):
        return lax.rem(dp + step, n_dp)

    def peer_loop(step):
        return lax.rem(loop + step, n_loop)

    barrier = pltpu.get_barrier_semaphore()
    for step in range(1, n_dp):
        pl.semaphore_signal(barrier, inc=1, device_id={"dp": peer_dp(step)}, device_id_type=pl.DeviceIdType.MESH)
    for step in range(1, n_loop):
        pl.semaphore_signal(barrier, inc=1, device_id={"loop": peer_loop(step)}, device_id_type=pl.DeviceIdType.MESH)

    loads = [
        pltpu.make_async_copy(source, target, load_sem.at[i])
        for i, (source, target) in enumerate((
            (text_hbm, own.at[TEXT]),
            (image_hbm, own.at[IMAGE]),
        ))
    ]
    for load in loads:
        load.start()

    def normalize(kind):
        loads[kind].wait()
        floats = own[kind].astype(jnp.float32)
        r = inverse_norm(floats)
        units[kind, 0] = (floats * r).astype(jnp.bfloat16)
        norms[kind] = r

    def piece(kind, part):
        size = rows // CHUNKS[kind]
        return pl.ds(part * size, size)

    def copy(kind, part, from_slot, to_slot, target, sem):
        return pltpu.make_async_remote_copy(
            src_ref=units.at[kind, from_slot, piece(kind, part)],
            dst_ref=units.at[kind, to_slot, piece(kind, part)],
            send_sem=sem.at[kind, to_slot, part],
            recv_sem=recv_sem.at[kind, to_slot, part],
            device_id={"dp": target},
            device_id_type=pl.DeviceIdType.MESH,
        )

    sent = []

    def send(kind, part):
        copies = [copy(kind, part, 0, 2 * k, peer_dp(2 * k), send_sem) for k in range(1, chips)]
        for c in copies:
            c.start()
        return copies

    def send_sibling(kind):
        for part in range(CHUNKS[kind]):
            sent.append(copy(kind, part, 0, 1, sibling, send_sem))
            sent[-1].start()

    def leave(copies):
        for c in copies:
            c.wait_send()

    def arrival(kind, part, slot):
        return copy(kind, part, 0, slot, sibling, send_sem)

    def pass_on(kind, part):
        for k in range(1, chips):
            arrival(kind, part, 2 * k).wait_recv()
            sent.append(copy(kind, part, 2 * k, 2 * k + 1, sibling, pass_sem))
            sent[-1].start()

    normalize(TEXT)
    pl.semaphore_wait(barrier, n_dp + n_loop - 2)
    texts_out = [c for part in range(CHUNKS[TEXT]) for c in send(TEXT, part)]
    send_sibling(TEXT)
    normalize(IMAGE)
    send_sibling(IMAGE)

    temper = jnp.exp(jnp.full((1, 128), scale_ref[0], jnp.float32))[:, :1]
    offset = bias_ref[0]
    image_unit = units[IMAGE, 0]
    text_unit = units[TEXT, 0]

    def eye():
        ids = lax.broadcasted_iota(jnp.int32, (rows, rows), 0)
        return ids == lax.broadcasted_iota(jnp.int32, (rows, rows), 1)

    sums = [jnp.zeros((rows, 128), jnp.float32) for _ in range(3)]

    def folded(values):
        return sum(values[:, c:c + 128] for c in range(0, values.shape[1], 128))

    def row_pair(k, first):
        texts = units[TEXT, 2 * k:2 * k + 2].reshape(2 * rows, -1)
        scaled = temper * dot_nt(image_unit, texts)
        logits = scaled + offset
        losses, coef = softplus_and_sigmoid(logits)
        if first:
            wide = jnp.concatenate([eye(), jnp.zeros((rows, rows), jnp.bool_)], axis=1)
            losses = jnp.where(wide, losses - logits, losses)
            coef = jnp.where(wide, coef - 1.0, coef)
        for i, values in enumerate((losses, coef * scaled, coef)):
            sums[i] += folded(values)
        return jnp.dot(coef.astype(jnp.bfloat16), texts, preferred_element_type=jnp.float32)

    def col_part(images, diagonal):
        logits = temper * dot_nt(text_unit, images) + offset
        _, coef = softplus_and_sigmoid(logits)
        if diagonal:
            coef = jnp.where(eye(), coef - 1.0, coef)
        return jnp.dot(coef.astype(jnp.bfloat16), images, preferred_element_type=jnp.float32)

    for part in range(CHUNKS[TEXT]):
        arrival(TEXT, part, 1).wait_recv()
    total[...] = row_pair(0, True)
    leave(texts_out)
    images_out = send(IMAGE, 0)
    for part in range(CHUNKS[TEXT]):
        pass_on(TEXT, part)
    for k in range(1, chips):
        for part in range(CHUNKS[TEXT]):
            arrival(TEXT, part, 2 * k + 1).wait_recv()
        total[...] += row_pair(k, False)

    def exchange(stage, buffer, count, target, axis):
        copies = []
        for step in range(1, count):
            copies.append(pltpu.make_async_remote_copy(
                src_ref=buffer.at[0],
                dst_ref=buffer.at[step],
                send_sem=sum_send.at[stage, step],
                recv_sem=sum_recv.at[stage, step],
                device_id={axis: target(step)},
                device_id_type=pl.DeviceIdType.MESH,
            ))
            copies[-1].start()
        return copies

    dp_sums[0] = jnp.concatenate(
        [jnp.sum(s, axis=0, keepdims=True) for s in sums] + [jnp.zeros((5, 128), jnp.float32)], axis=0
    )
    dp_copies = exchange(0, dp_sums, n_dp, peer_dp, "dp")

    leave(images_out)
    images_out = send(IMAGE, 1)
    image_grad_ref[...] = unit_pull(own[IMAGE], norms[IMAGE], total[...], temper)

    total[...] = col_part(image_unit, True)
    for part in range(CHUNKS[IMAGE]):
        arrival(IMAGE, part, 1).wait_recv()
    total[...] += col_part(units[IMAGE, 1], False)

    for c in dp_copies:
        c.wait_recv()
    loop_sums[0] = jnp.sum(dp_sums[...], axis=0)
    loop_copies = exchange(1, loop_sums, n_loop, peer_loop, "loop")

    for part in range(CHUNKS[IMAGE]):
        pass_on(IMAGE, part)
        for k in range(1, chips):
            total[...] += col_part(units[IMAGE, 2 * k, piece(IMAGE, part)], False)
            arrival(IMAGE, part, 2 * k + 1).wait_recv()
            total[...] += col_part(units[IMAGE, 2 * k + 1, piece(IMAGE, part)], False)
    text_grad_ref[...] = unit_pull(own[TEXT], norms[TEXT], total[...], temper)

    for c in loop_copies:
        c.wait_recv()
    sums_ref[...] = jnp.sum(loop_sums[...], axis=0)

    leave(sent + images_out + dp_copies + loop_copies)


def finish(
    inverse_batch, image_grad, text_grad, sums_ref,
    loss_ref, image_grad_hbm, text_grad_hbm, scale_grad_ref, bias_grad_ref, sems,
):
    stores = [
        pltpu.make_async_copy(image_grad, image_grad_hbm, sems.at[0]),
        pltpu.make_async_copy(text_grad, text_grad_hbm, sems.at[1]),
    ]
    for store in stores:
        store.start()
    loss_ref[0] = jnp.sum(sums_ref[0:1, :]) * inverse_batch
    scale_grad_ref[0] = jnp.sum(sums_ref[1:2, :])
    bias_grad_ref[0] = jnp.sum(sums_ref[2:3, :])
    for store in stores:
        store.wait()


def solution(mesh):
    n_dp, n_loop = mesh.shape["dp"], mesh.shape["loop"]

    def on_device(image_embeds, text_embeds, log_scale, logit_bias):
        rows, width = image_embeds.shape
        scalar = jax.ShapeDtypeStruct((1,), jnp.float32)
        grad = jax.ShapeDtypeStruct((rows, width), jnp.bfloat16)
        hbm = pl.BlockSpec(memory_space=pltpu.HBM)
        vmem = pl.BlockSpec(memory_space=pltpu.VMEM)
        smem = pl.BlockSpec(memory_space=pltpu.SMEM)
        parts = max(CHUNKS)
        image_grad, text_grad, sums = pl.pallas_call(
            functools.partial(kernel, n_dp, n_loop),
            out_shape=(
                pltpu.VMEM((rows, width), jnp.bfloat16),
                pltpu.VMEM((rows, width), jnp.bfloat16),
                pltpu.VMEM((8, 128), jnp.float32),
            ),
            in_specs=[hbm, hbm, smem, smem],
            out_specs=(vmem, vmem, vmem),
            scratch_shapes=[
                pltpu.VMEM((2, rows, width), jnp.bfloat16),
                pltpu.VMEM((2, n_dp, rows, width), jnp.bfloat16),
                pltpu.VMEM((rows, width), jnp.float32),
                pltpu.VMEM((2, rows, 1), jnp.float32),
                pltpu.VMEM((n_dp, 8, 128), jnp.float32),
                pltpu.VMEM((n_loop, 8, 128), jnp.float32),
                pltpu.SemaphoreType.DMA((2,)),
                pltpu.SemaphoreType.DMA((2, n_dp, parts)),
                pltpu.SemaphoreType.DMA((2, n_dp, parts)),
                pltpu.SemaphoreType.DMA((2, n_dp, parts)),
                pltpu.SemaphoreType.DMA((2, max(n_dp, n_loop))),
                pltpu.SemaphoreType.DMA((2, max(n_dp, n_loop))),
            ],
            compiler_params=pltpu.CompilerParams(
                collective_id=0, has_side_effects=True, vmem_limit_bytes=32 * 1024 * 1024
            ),
        )(
            pltpu.with_memory_space_constraint(image_embeds, pltpu.HBM),
            pltpu.with_memory_space_constraint(text_embeds, pltpu.HBM),
            log_scale,
            logit_bias,
        )
        return pl.pallas_call(
            functools.partial(finish, 1.0 / (rows * n_dp * n_loop)),
            out_shape=(scalar, grad, grad, scalar, scalar),
            in_specs=[vmem] * 3,
            out_specs=(smem, hbm, hbm, smem, smem),
            scratch_shapes=[pltpu.SemaphoreType.DMA((2,))],
        )(image_grad, text_grad, sums)

    return jax.shard_map(
        on_device,
        mesh=mesh,
        in_specs=(P(("dp", "loop"), None), P(("dp", "loop"), None), P(), P()),
        out_specs=(P(), P(("dp", "loop"), None), P(("dp", "loop"), None), P(), P()),
        check_vma=False,
    )
```

```python
import functools

import jax
import jax.numpy as jnp
from jax import lax
from jax.experimental import pallas as pl
from jax.experimental.pallas import tpu as pltpu
from jax.sharding import PartitionSpec as P

EPSILON = 1e-06
TEXT, IMAGE = 0, 1
CUTS = ((0, 4, 8), (0, 3, 6, 8))
CHUNKS = tuple(len(cuts) - 1 for cuts in CUTS)


def inverse_norm(floats):
    return lax.rsqrt(jnp.sum(floats * floats, axis=1, keepdims=True) + EPSILON)


def softplus_and_sigmoid(logits):
    small = jnp.exp(-jnp.abs(logits))
    softplus = jnp.maximum(logits, 0.0) + jnp.log1p(small)
    sigmoid = jnp.where(logits >= 0.0, 1.0, small) / (1.0 + small)
    return softplus, sigmoid


def dot_nt(left, right):
    return lax.dot_general(
        left, right, (((1,), (1,)), ((), ())), preferred_element_type=jnp.float32
    )


def unit_pull(embeds, r, cot, temper):
    floats = embeds.astype(jnp.float32)
    along = jnp.sum(floats * cot, axis=1, keepdims=True)
    return ((temper * r) * (cot - floats * (r * r * along))).astype(jnp.bfloat16)


def kernel(
    n_dp, n_loop,
    image_hbm, text_hbm, scale_ref, bias_ref,
    image_grad_ref, text_grad_ref, sums_ref,
    raw, own_image, units, total, norms, dp_sums, loop_sums,
    load_sem, send_sem, recv_sem, pass_sem, sum_send, sum_recv,
):
    rows = own_image.shape[0]
    chips = n_dp // 2
    dp, loop = lax.axis_index("dp"), lax.axis_index("loop")
    core = lax.rem(dp, 2)
    sibling = dp + 1 - 2 * core

    def peer_dp(step):
        return lax.rem(dp + step, n_dp)

    def peer_loop(step):
        return lax.rem(loop + step, n_loop)

    barrier = pltpu.get_barrier_semaphore()
    for step in range(1, n_dp):
        pl.semaphore_signal(barrier, inc=1, device_id={"dp": peer_dp(step)}, device_id_type=pl.DeviceIdType.MESH)
    for step in range(1, n_loop):
        pl.semaphore_signal(barrier, inc=1, device_id={"loop": peer_loop(step)}, device_id_type=pl.DeviceIdType.MESH)

    loads = [
        pltpu.make_async_copy(text_hbm, raw.at[0], load_sem.at[TEXT]),
        pltpu.make_async_copy(image_hbm, own_image, load_sem.at[IMAGE]),
    ]
    for load in loads:
        load.start()

    def normalize(kind, slot, embeds):
        floats = embeds.astype(jnp.float32)
        r = inverse_norm(floats)
        units[kind, slot] = (floats * r).astype(jnp.bfloat16)
        return r

    def piece(kind, part):
        first, last = CUTS[kind][part] * rows // 8, CUTS[kind][part + 1] * rows // 8
        return pl.ds(first, last - first)

    def block(kind, slot):
        return raw.at[slot] if kind == TEXT else units.at[IMAGE, slot]

    def copy(kind, part, source, to_slot, target, sem):
        return pltpu.make_async_remote_copy(
            src_ref=source.at[piece(kind, part)],
            dst_ref=block(kind, to_slot).at[piece(kind, part)],
            send_sem=sem.at[kind, to_slot, part],
            recv_sem=recv_sem.at[kind, to_slot, part],
            device_id={"dp": target},
            device_id_type=pl.DeviceIdType.MESH,
        )

    sources = (text_hbm, units.at[IMAGE, 0])
    sent = []

    def send(kind, part):
        copies = [copy(kind, part, sources[kind], 2 * k, peer_dp(2 * k), send_sem) for k in range(1, chips)]
        for c in copies:
            c.start()
        return copies

    def send_sibling(kind):
        for part in range(CHUNKS[kind]):
            sent.append(copy(kind, part, sources[kind], 1, sibling, send_sem))
            sent[-1].start()

    def leave(copies):
        for c in copies:
            c.wait_send()

    def arrival(kind, part, slot):
        return copy(kind, part, sources[kind], slot, sibling, send_sem)

    def pass_on(kind, part):
        for k in range(1, chips):
            arrival(kind, part, 2 * k).wait_recv()
            sent.append(copy(kind, part, block(kind, 2 * k), 2 * k + 1, sibling, pass_sem))
            sent[-1].start()

    pl.semaphore_wait(barrier, n_dp + n_loop - 2)
    texts_out = [c for part in range(CHUNKS[TEXT]) for c in send(TEXT, part)]
    send_sibling(TEXT)
    loads[IMAGE].wait()
    norms[IMAGE] = normalize(IMAGE, 0, own_image[...])
    send_sibling(IMAGE)
    loads[TEXT].wait()
    norms[TEXT] = normalize(TEXT, 0, raw[0])

    temper = jnp.exp(jnp.full((1, 128), scale_ref[0], jnp.float32))[:, :1]
    offset = bias_ref[0]
    image_unit = units[IMAGE, 0]
    text_unit = units[TEXT, 0]

    def eye():
        ids = lax.broadcasted_iota(jnp.int32, (rows, rows), 0)
        return ids == lax.broadcasted_iota(jnp.int32, (rows, rows), 1)

    sums = [jnp.zeros((rows, 128), jnp.float32) for _ in range(3)]

    def folded(values):
        return sum(values[:, c:c + 128] for c in range(0, values.shape[1], 128))

    def row_pair(k, first):
        texts = units[TEXT, 2 * k:2 * k + 2].reshape(2 * rows, -1)
        scaled = temper * dot_nt(image_unit, texts)
        logits = scaled + offset
        losses, coef = softplus_and_sigmoid(logits)
        if first:
            wide = jnp.concatenate([eye(), jnp.zeros((rows, rows), jnp.bool_)], axis=1)
            losses = jnp.where(wide, losses - logits, losses)
            coef = jnp.where(wide, coef - 1.0, coef)
        for i, values in enumerate((losses, coef * scaled, coef)):
            sums[i] += folded(values)
        return jnp.dot(coef.astype(jnp.bfloat16), texts, preferred_element_type=jnp.float32)

    def col_part(images, diagonal):
        logits = temper * dot_nt(text_unit, images) + offset
        _, coef = softplus_and_sigmoid(logits)
        if diagonal:
            coef = jnp.where(eye(), coef - 1.0, coef)
        return jnp.dot(coef.astype(jnp.bfloat16), images, preferred_element_type=jnp.float32)

    for part in range(CHUNKS[TEXT]):
        arrival(TEXT, part, 1).wait_recv()
    normalize(TEXT, 1, raw[1])
    total[...] = row_pair(0, True)
    leave(texts_out)
    images_out = [send(IMAGE, part) for part in range(2)]
    for part in range(CHUNKS[TEXT]):
        pass_on(TEXT, part)
    for k in range(1, chips):
        normalize(TEXT, 2 * k, raw[2 * k])
        for part in range(CHUNKS[TEXT]):
            arrival(TEXT, part, 2 * k + 1).wait_recv()
        normalize(TEXT, 2 * k + 1, raw[2 * k + 1])
        total[...] += row_pair(k, False)

    def exchange(stage, buffer, count, target, axis):
        copies = []
        for step in range(1, count):
            copies.append(pltpu.make_async_remote_copy(
                src_ref=buffer.at[0],
                dst_ref=buffer.at[step],
                send_sem=sum_send.at[stage, step],
                recv_sem=sum_recv.at[stage, step],
                device_id={axis: target(step)},
                device_id_type=pl.DeviceIdType.MESH,
            ))
            copies[-1].start()
        return copies

    dp_sums[0] = jnp.concatenate(
        [jnp.sum(s, axis=0, keepdims=True) for s in sums] + [jnp.zeros((5, 128), jnp.float32)], axis=0
    )
    dp_copies = exchange(0, dp_sums, n_dp, peer_dp, "dp")

    image_grad_ref[...] = unit_pull(own_image[...], norms[IMAGE], total[...], temper)
    leave(images_out[0])
    images_out.append(send(IMAGE, 2))

    total[...] = col_part(image_unit, True)
    for part in range(CHUNKS[IMAGE]):
        arrival(IMAGE, part, 1).wait_recv()
    total[...] += col_part(units[IMAGE, 1], False)

    for c in dp_copies:
        c.wait_recv()
    loop_sums[0] = jnp.sum(dp_sums[...], axis=0)
    loop_copies = exchange(1, loop_sums, n_loop, peer_loop, "loop")

    for part in range(CHUNKS[IMAGE]):
        pass_on(IMAGE, part)
        for k in range(1, chips):
            total[...] += col_part(units[IMAGE, 2 * k, piece(IMAGE, part)], False)
            arrival(IMAGE, part, 2 * k + 1).wait_recv()
            total[...] += col_part(units[IMAGE, 2 * k + 1, piece(IMAGE, part)], False)
    text_grad_ref[...] = unit_pull(raw[0], norms[TEXT], total[...], temper)

    for c in loop_copies:
        c.wait_recv()
    sums_ref[...] = jnp.sum(loop_sums[...], axis=0)

    leave(sent + images_out[1] + images_out[2] + dp_copies + loop_copies)


def finish(
    inverse_batch, image_grad, text_grad, sums_ref,
    loss_ref, image_grad_hbm, text_grad_hbm, scale_grad_ref, bias_grad_ref, sems,
):
    stores = [
        pltpu.make_async_copy(image_grad, image_grad_hbm, sems.at[0]),
        pltpu.make_async_copy(text_grad, text_grad_hbm, sems.at[1]),
    ]
    for store in stores:
        store.start()
    loss_ref[0] = jnp.sum(sums_ref[0:1, :]) * inverse_batch
    scale_grad_ref[0] = jnp.sum(sums_ref[1:2, :])
    bias_grad_ref[0] = jnp.sum(sums_ref[2:3, :])
    for store in stores:
        store.wait()


def solution(mesh):
    n_dp, n_loop = mesh.shape["dp"], mesh.shape["loop"]

    def on_device(image_embeds, text_embeds, log_scale, logit_bias):
        rows, width = image_embeds.shape
        scalar = jax.ShapeDtypeStruct((1,), jnp.float32)
        grad = jax.ShapeDtypeStruct((rows, width), jnp.bfloat16)
        hbm = pl.BlockSpec(memory_space=pltpu.HBM)
        vmem = pl.BlockSpec(memory_space=pltpu.VMEM)
        smem = pl.BlockSpec(memory_space=pltpu.SMEM)
        parts = max(CHUNKS)
        image_grad, text_grad, sums = pl.pallas_call(
            functools.partial(kernel, n_dp, n_loop),
            out_shape=(
                pltpu.VMEM((rows, width), jnp.bfloat16),
                pltpu.VMEM((rows, width), jnp.bfloat16),
                pltpu.VMEM((8, 128), jnp.float32),
            ),
            in_specs=[hbm, hbm, smem, smem],
            out_specs=(vmem, vmem, vmem),
            scratch_shapes=[
                pltpu.VMEM((n_dp, rows, width), jnp.bfloat16),
                pltpu.VMEM((rows, width), jnp.bfloat16),
                pltpu.VMEM((2, n_dp, rows, width), jnp.bfloat16),
                pltpu.VMEM((rows, width), jnp.float32),
                pltpu.VMEM((2, rows, 1), jnp.float32),
                pltpu.VMEM((n_dp, 8, 128), jnp.float32),
                pltpu.VMEM((n_loop, 8, 128), jnp.float32),
                pltpu.SemaphoreType.DMA((2,)),
                pltpu.SemaphoreType.DMA((2, n_dp, parts)),
                pltpu.SemaphoreType.DMA((2, n_dp, parts)),
                pltpu.SemaphoreType.DMA((2, n_dp, parts)),
                pltpu.SemaphoreType.DMA((2, max(n_dp, n_loop))),
                pltpu.SemaphoreType.DMA((2, max(n_dp, n_loop))),
            ],
            compiler_params=pltpu.CompilerParams(
                collective_id=0, has_side_effects=True, vmem_limit_bytes=32 * 1024 * 1024
            ),
        )(
            pltpu.with_memory_space_constraint(image_embeds, pltpu.HBM),
            pltpu.with_memory_space_constraint(text_embeds, pltpu.HBM),
            log_scale,
            logit_bias,
        )
        return pl.pallas_call(
            functools.partial(finish, 1.0 / (rows * n_dp * n_loop)),
            out_shape=(scalar, grad, grad, scalar, scalar),
            in_specs=[vmem] * 3,
            out_specs=(smem, hbm, hbm, smem, smem),
            scratch_shapes=[pltpu.SemaphoreType.DMA((2,))],
            compiler_params=pltpu.CompilerParams(vmem_limit_bytes=4 * 1024 * 1024),
        )(image_grad, text_grad, sums)

    return jax.shard_map(
        on_device,
        mesh=mesh,
        in_specs=(P(("dp", "loop"), None), P(("dp", "loop"), None), P(), P()),
        out_specs=(P(), P(("dp", "loop"), None), P(("dp", "loop"), None), P(), P()),
        check_vma=False,
    )
```

```python
import functools

import jax
import jax.numpy as jnp
from jax import lax
from jax.experimental import pallas as pl
from jax.experimental.pallas import tpu as pltpu
from jax.sharding import PartitionSpec as P

EPSILON = 1e-06
TEXT, IMAGE = 0, 1
CUTS = ((0, 4, 8), (0, 5, 8))
CHUNKS = tuple(len(cuts) - 1 for cuts in CUTS)


def inverse_norm(floats):
    return lax.rsqrt(jnp.sum(floats * floats, axis=1, keepdims=True) + EPSILON)


def softplus_and_sigmoid(logits):
    small = jnp.exp(-jnp.abs(logits))
    softplus = jnp.maximum(logits, 0.0) + jnp.log1p(small)
    sigmoid = jnp.where(logits >= 0.0, 1.0, small) / (1.0 + small)
    return softplus, sigmoid


def dot_nt(left, right):
    return lax.dot_general(
        left, right, (((1,), (1,)), ((), ())), preferred_element_type=jnp.float32
    )


def unit_pull(embeds, r, cot, temper):
    floats = embeds.astype(jnp.float32)
    along = jnp.sum(floats * cot, axis=1, keepdims=True)
    return ((temper * r) * (cot - floats * (r * r * along))).astype(jnp.bfloat16)


def kernel(
    n_dp, n_loop,
    image_hbm, text_hbm, scale_ref, bias_ref,
    image_grad_ref, text_grad_ref, sums_ref,
    raw, own_image, units, total, norms, dp_sums, loop_sums,
    load_sem, send_sem, recv_sem, pass_sem, sum_send, sum_recv,
):
    rows = own_image.shape[0]
    chips = n_dp // 2
    dp, loop = lax.axis_index("dp"), lax.axis_index("loop")
    core = lax.rem(dp, 2)
    sibling = dp + 1 - 2 * core

    def peer_dp(step):
        return lax.rem(dp + step, n_dp)

    def peer_loop(step):
        return lax.rem(loop + step, n_loop)

    barrier = pltpu.get_barrier_semaphore()
    for step in range(1, n_dp):
        pl.semaphore_signal(barrier, inc=1, device_id={"dp": peer_dp(step)}, device_id_type=pl.DeviceIdType.MESH)
    for step in range(1, n_loop):
        pl.semaphore_signal(barrier, inc=1, device_id={"loop": peer_loop(step)}, device_id_type=pl.DeviceIdType.MESH)

    loads = [
        pltpu.make_async_copy(text_hbm, raw.at[0], load_sem.at[TEXT]),
        pltpu.make_async_copy(image_hbm, own_image, load_sem.at[IMAGE]),
    ]
    for load in loads:
        load.start()

    def normalize(kind, slot, embeds):
        floats = embeds.astype(jnp.float32)
        r = inverse_norm(floats)
        units[kind, slot] = (floats * r).astype(jnp.bfloat16)
        return r

    def piece(kind, part):
        first, last = CUTS[kind][part] * rows // 8, CUTS[kind][part + 1] * rows // 8
        return pl.ds(first, last - first)

    def block(kind, slot):
        return raw.at[slot] if kind == TEXT else units.at[IMAGE, slot]

    def copy(kind, part, source, to_slot, target, sem):
        return pltpu.make_async_remote_copy(
            src_ref=source.at[piece(kind, part)],
            dst_ref=block(kind, to_slot).at[piece(kind, part)],
            send_sem=sem.at[kind, to_slot, part],
            recv_sem=recv_sem.at[kind, to_slot, part],
            device_id={"dp": target},
            device_id_type=pl.DeviceIdType.MESH,
        )

    sources = (text_hbm, units.at[IMAGE, 0])
    sent = []

    def send(kind, part):
        copies = [copy(kind, part, sources[kind], 2 * k, peer_dp(2 * k), send_sem) for k in range(1, chips)]
        for c in copies:
            c.start()
        return copies

    def send_sibling(kind):
        for part in range(CHUNKS[kind]):
            sent.append(copy(kind, part, sources[kind], 1, sibling, send_sem))
            sent[-1].start()

    def leave(copies):
        for c in copies:
            c.wait_send()

    def arrival(kind, part, slot):
        return copy(kind, part, sources[kind], slot, sibling, send_sem)

    def pass_on(kind, part):
        for k in range(1, chips):
            arrival(kind, part, 2 * k).wait_recv()
            sent.append(copy(kind, part, block(kind, 2 * k), 2 * k + 1, sibling, pass_sem))
            sent[-1].start()

    pl.semaphore_wait(barrier, n_dp + n_loop - 2)
    texts_out = [c for part in range(CHUNKS[TEXT]) for c in send(TEXT, part)]
    send_sibling(TEXT)
    loads[IMAGE].wait()
    norms[IMAGE] = normalize(IMAGE, 0, own_image[...])
    send_sibling(IMAGE)
    loads[TEXT].wait()
    norms[TEXT] = normalize(TEXT, 0, raw[0])

    temper = jnp.exp(jnp.full((1, 128), scale_ref[0], jnp.float32))[:, :1]
    offset = bias_ref[0]
    image_unit = units[IMAGE, 0]
    text_unit = units[TEXT, 0]

    def eye():
        ids = lax.broadcasted_iota(jnp.int32, (rows, rows), 0)
        return ids == lax.broadcasted_iota(jnp.int32, (rows, rows), 1)

    sums = [jnp.zeros((rows, 128), jnp.float32) for _ in range(3)]

    def folded(values):
        return sum(values[:, c:c + 128] for c in range(0, values.shape[1], 128))

    def less_eye(values, subtrahend):
        wide = jnp.concatenate([eye(), jnp.zeros((rows, rows), jnp.bool_)], axis=1)
        return jnp.where(wide, values - subtrahend, values)

    def row_pair(k, first):
        texts = units[TEXT, 2 * k:2 * k + 2].reshape(2 * rows, -1)
        scaled = temper * dot_nt(image_unit, texts)
        logits = scaled + offset
        losses, coef = softplus_and_sigmoid(logits)
        if first:
            losses = less_eye(losses, logits)
            coef = less_eye(coef, 1.0)
        for i, values in enumerate((losses, coef * scaled, coef)):
            sums[i] += folded(values)
        return jnp.dot(coef.astype(jnp.bfloat16), texts, preferred_element_type=jnp.float32)

    def col_part(images, first):
        logits = temper * dot_nt(text_unit, images) + offset
        _, coef = softplus_and_sigmoid(logits)
        if first:
            coef = less_eye(coef, 1.0)
        return jnp.dot(coef.astype(jnp.bfloat16), images, preferred_element_type=jnp.float32)

    def image_pair(k, part):
        return units[IMAGE, 2 * k:2 * k + 2, piece(IMAGE, part)].reshape(-1, units.shape[3])

    for part in range(CHUNKS[TEXT]):
        arrival(TEXT, part, 1).wait_recv()
    normalize(TEXT, 1, raw[1])
    total[IMAGE] = row_pair(0, True)
    for part in range(CHUNKS[IMAGE]):
        arrival(IMAGE, part, 1).wait_recv()
    total[TEXT] = col_part(units[IMAGE, 0:2].reshape(2 * rows, -1), True)
    leave(texts_out)
    images_out = [c for part in range(CHUNKS[IMAGE]) for c in send(IMAGE, part)]
    for part in range(CHUNKS[TEXT]):
        pass_on(TEXT, part)
    for k in range(1, chips):
        normalize(TEXT, 2 * k, raw[2 * k])
        for part in range(CHUNKS[TEXT]):
            arrival(TEXT, part, 2 * k + 1).wait_recv()
        normalize(TEXT, 2 * k + 1, raw[2 * k + 1])
        total[IMAGE] += row_pair(k, False)

    def exchange(stage, buffer, count, target, axis):
        copies = []
        for step in range(1, count):
            copies.append(pltpu.make_async_remote_copy(
                src_ref=buffer.at[0],
                dst_ref=buffer.at[step],
                send_sem=sum_send.at[stage, step],
                recv_sem=sum_recv.at[stage, step],
                device_id={axis: target(step)},
                device_id_type=pl.DeviceIdType.MESH,
            ))
            copies[-1].start()
        return copies

    dp_sums[0] = jnp.concatenate(
        [jnp.sum(s, axis=0, keepdims=True) for s in sums] + [jnp.zeros((5, 128), jnp.float32)], axis=0
    )
    dp_copies = exchange(0, dp_sums, n_dp, peer_dp, "dp")

    image_grad_ref[...] = unit_pull(own_image[...], norms[IMAGE], total[IMAGE], temper)

    pass_on(IMAGE, 0)
    for c in dp_copies:
        c.wait_recv()
    loop_sums[0] = jnp.sum(dp_sums[...], axis=0)
    loop_copies = exchange(1, loop_sums, n_loop, peer_loop, "loop")
    for part in range(CHUNKS[IMAGE] - 1):
        for k in range(1, chips):
            arrival(IMAGE, part, 2 * k + 1).wait_recv()
            total[TEXT] += col_part(image_pair(k, part), False)
        pass_on(IMAGE, part + 1)
    last = CHUNKS[IMAGE] - 1
    for k in range(1, chips):
        total[TEXT] += col_part(units[IMAGE, 2 * k, piece(IMAGE, last)], False)
    for k in range(1, chips):
        arrival(IMAGE, last, 2 * k + 1).wait_recv()
        total[TEXT] += col_part(units[IMAGE, 2 * k + 1, piece(IMAGE, last)], False)
    text_grad_ref[...] = unit_pull(raw[0], norms[TEXT], total[TEXT], temper)

    for c in loop_copies:
        c.wait_recv()
    sums_ref[...] = jnp.sum(loop_sums[...], axis=0)

    leave(sent + images_out + dp_copies + loop_copies)


def finish(
    inverse_batch, image_grad, text_grad, sums_ref,
    loss_ref, image_grad_hbm, text_grad_hbm, scale_grad_ref, bias_grad_ref, sems,
):
    stores = [
        pltpu.make_async_copy(image_grad, image_grad_hbm, sems.at[0]),
        pltpu.make_async_copy(text_grad, text_grad_hbm, sems.at[1]),
    ]
    for store in stores:
        store.start()
    loss_ref[0] = jnp.sum(sums_ref[0:1, :]) * inverse_batch
    scale_grad_ref[0] = jnp.sum(sums_ref[1:2, :])
    bias_grad_ref[0] = jnp.sum(sums_ref[2:3, :])
    for store in stores:
        store.wait()


def solution(mesh):
    n_dp, n_loop = mesh.shape["dp"], mesh.shape["loop"]

    def on_device(image_embeds, text_embeds, log_scale, logit_bias):
        rows, width = image_embeds.shape
        scalar = jax.ShapeDtypeStruct((1,), jnp.float32)
        grad = jax.ShapeDtypeStruct((rows, width), jnp.bfloat16)
        hbm = pl.BlockSpec(memory_space=pltpu.HBM)
        vmem = pl.BlockSpec(memory_space=pltpu.VMEM)
        smem = pl.BlockSpec(memory_space=pltpu.SMEM)
        parts = max(CHUNKS)
        image_grad, text_grad, sums = pl.pallas_call(
            functools.partial(kernel, n_dp, n_loop),
            out_shape=(
                pltpu.VMEM((rows, width), jnp.bfloat16),
                pltpu.VMEM((rows, width), jnp.bfloat16),
                pltpu.VMEM((8, 128), jnp.float32),
            ),
            in_specs=[hbm, hbm, smem, smem],
            out_specs=(vmem, vmem, vmem),
            scratch_shapes=[
                pltpu.VMEM((n_dp, rows, width), jnp.bfloat16),
                pltpu.VMEM((rows, width), jnp.bfloat16),
                pltpu.VMEM((2, n_dp, rows, width), jnp.bfloat16),
                pltpu.VMEM((2, rows, width), jnp.float32),
                pltpu.VMEM((2, rows, 1), jnp.float32),
                pltpu.VMEM((n_dp, 8, 128), jnp.float32),
                pltpu.VMEM((n_loop, 8, 128), jnp.float32),
                pltpu.SemaphoreType.DMA((2,)),
                pltpu.SemaphoreType.DMA((2, n_dp, parts)),
                pltpu.SemaphoreType.DMA((2, n_dp, parts)),
                pltpu.SemaphoreType.DMA((2, n_dp, parts)),
                pltpu.SemaphoreType.DMA((2, max(n_dp, n_loop))),
                pltpu.SemaphoreType.DMA((2, max(n_dp, n_loop))),
            ],
            compiler_params=pltpu.CompilerParams(
                collective_id=0, has_side_effects=True, vmem_limit_bytes=32 * 1024 * 1024
            ),
        )(
            pltpu.with_memory_space_constraint(image_embeds, pltpu.HBM),
            pltpu.with_memory_space_constraint(text_embeds, pltpu.HBM),
            log_scale,
            logit_bias,
        )
        return pl.pallas_call(
            functools.partial(finish, 1.0 / (rows * n_dp * n_loop)),
            out_shape=(scalar, grad, grad, scalar, scalar),
            in_specs=[vmem] * 3,
            out_specs=(smem, hbm, hbm, smem, smem),
            scratch_shapes=[pltpu.SemaphoreType.DMA((2,))],
            compiler_params=pltpu.CompilerParams(vmem_limit_bytes=4 * 1024 * 1024),
        )(image_grad, text_grad, sums)

    return jax.shard_map(
        on_device,
        mesh=mesh,
        in_specs=(P(("dp", "loop"), None), P(("dp", "loop"), None), P(), P()),
        out_specs=(P(), P(("dp", "loop"), None), P(("dp", "loop"), None), P(), P()),
        check_vma=False,
    )
```

```python
import functools

import jax
import jax.numpy as jnp
from jax import lax
from jax.experimental import pallas as pl
from jax.experimental.pallas import tpu as pltpu
from jax.sharding import PartitionSpec as P

EPSILON = 1e-06
TEXT, IMAGE = 0, 1
CUTS = ((0, 4, 8), (0, 5, 8))
CHUNKS = tuple(len(cuts) - 1 for cuts in CUTS)


def inverse_norm(floats):
    return lax.rsqrt(jnp.sum(floats * floats, axis=1, keepdims=True) + EPSILON)


def softplus_and_sigmoid(logits):
    small = jnp.exp(-jnp.abs(logits))
    softplus = jnp.maximum(logits, 0.0) + jnp.log1p(small)
    sigmoid = jnp.where(logits >= 0.0, 1.0, small) / (1.0 + small)
    return softplus, sigmoid


def dot_nt(left, right):
    return lax.dot_general(
        left, right, (((1,), (1,)), ((), ())), preferred_element_type=jnp.float32
    )


def unit_pull(embeds, r, cot, temper):
    floats = embeds.astype(jnp.float32)
    along = jnp.sum(floats * cot, axis=1, keepdims=True)
    return ((temper * r) * (cot - floats * (r * r * along))).astype(jnp.bfloat16)


def kernel(
    n_dp, n_loop,
    image_hbm, text_hbm, scale_ref, bias_ref,
    image_grad_ref, text_grad_ref, sums_ref,
    own, units, total, norms, dp_sums, loop_sums,
    load_sem, send_sem, recv_sem, pass_sem, sum_send, sum_recv,
):
    rows = own.shape[1]
    chips = n_dp // 2
    dp, loop = lax.axis_index("dp"), lax.axis_index("loop")
    core = lax.rem(dp, 2)
    sibling = dp + 1 - 2 * core

    def peer_dp(step):
        return lax.rem(dp + step, n_dp)

    def peer_loop(step):
        return lax.rem(loop + step, n_loop)

    barrier = pltpu.get_barrier_semaphore()
    for step in range(1, n_dp):
        pl.semaphore_signal(barrier, inc=1, device_id={"dp": peer_dp(step)}, device_id_type=pl.DeviceIdType.MESH)
    for step in range(1, n_loop):
        pl.semaphore_signal(barrier, inc=1, device_id={"loop": peer_loop(step)}, device_id_type=pl.DeviceIdType.MESH)

    loads = [
        pltpu.make_async_copy(text_hbm, own.at[TEXT], load_sem.at[TEXT]),
        pltpu.make_async_copy(image_hbm, own.at[IMAGE], load_sem.at[IMAGE]),
    ]
    for load in loads:
        load.start()

    def normalize(kind):
        loads[kind].wait()
        floats = own[kind].astype(jnp.float32)
        r = inverse_norm(floats)
        units[kind, 0] = (floats * r).astype(jnp.bfloat16)
        norms[kind] = r

    def piece(kind, part):
        first, last = CUTS[kind][part] * rows // 8, CUTS[kind][part + 1] * rows // 8
        return pl.ds(first, last - first)

    def copy(kind, part, from_slot, to_slot, target, sem):
        return pltpu.make_async_remote_copy(
            src_ref=units.at[kind, from_slot, piece(kind, part)],
            dst_ref=units.at[kind, to_slot, piece(kind, part)],
            send_sem=sem.at[kind, to_slot, part],
            recv_sem=recv_sem.at[kind, to_slot, part],
            device_id={"dp": target},
            device_id_type=pl.DeviceIdType.MESH,
        )

    sent = []

    def send(kind, part):
        copies = [copy(kind, part, 0, 2 * k, peer_dp(2 * k), send_sem) for k in range(1, chips)]
        for c in copies:
            c.start()
        return copies

    def send_sibling(kind):
        for part in range(CHUNKS[kind]):
            sent.append(copy(kind, part, 0, 1, sibling, send_sem))
            sent[-1].start()

    def leave(copies):
        for c in copies:
            c.wait_send()

    def arrival(kind, part, slot):
        return copy(kind, part, 0, slot, sibling, send_sem)

    def pass_on(kind, part):
        for k in range(1, chips):
            arrival(kind, part, 2 * k).wait_recv()
            sent.append(copy(kind, part, 2 * k, 2 * k + 1, sibling, pass_sem))
            sent[-1].start()

    normalize(TEXT)
    pl.semaphore_wait(barrier, n_dp + n_loop - 2)
    texts_out = [c for part in range(CHUNKS[TEXT]) for c in send(TEXT, part)]
    send_sibling(TEXT)
    normalize(IMAGE)
    send_sibling(IMAGE)

    temper = jnp.exp(jnp.full((1, 128), scale_ref[0], jnp.float32))[:, :1]
    offset = bias_ref[0]
    image_unit = units[IMAGE, 0]
    text_unit = units[TEXT, 0]

    def eye():
        ids = lax.broadcasted_iota(jnp.int32, (rows, rows), 0)
        return ids == lax.broadcasted_iota(jnp.int32, (rows, rows), 1)

    sums = [jnp.zeros((rows, 128), jnp.float32) for _ in range(3)]

    def folded(values):
        return sum(values[:, c:c + 128] for c in range(0, values.shape[1], 128))

    def less_eye(values, subtrahend):
        wide = jnp.concatenate([eye(), jnp.zeros((rows, rows), jnp.bool_)], axis=1)
        return jnp.where(wide, values - subtrahend, values)

    def row_pair(k, first):
        texts = units[TEXT, 2 * k:2 * k + 2].reshape(2 * rows, -1)
        scaled = temper * dot_nt(image_unit, texts)
        logits = scaled + offset
        losses, coef = softplus_and_sigmoid(logits)
        if first:
            losses = less_eye(losses, logits)
            coef = less_eye(coef, 1.0)
        for i, values in enumerate((losses, coef * scaled, coef)):
            sums[i] += folded(values)
        return jnp.dot(coef.astype(jnp.bfloat16), texts, preferred_element_type=jnp.float32)

    def col_part(images, first):
        logits = temper * dot_nt(text_unit, images) + offset
        _, coef = softplus_and_sigmoid(logits)
        if first:
            coef = less_eye(coef, 1.0)
        return jnp.dot(coef.astype(jnp.bfloat16), images, preferred_element_type=jnp.float32)

    def image_pair(k, part):
        return units[IMAGE, 2 * k:2 * k + 2, piece(IMAGE, part)].reshape(-1, units.shape[3])

    for part in range(CHUNKS[TEXT]):
        arrival(TEXT, part, 1).wait_recv()
    total[IMAGE] = row_pair(0, True)
    for part in range(CHUNKS[IMAGE]):
        arrival(IMAGE, part, 1).wait_recv()
    total[TEXT] = col_part(units[IMAGE, 0:2].reshape(2 * rows, -1), True)
    leave(texts_out)
    images_out = send(IMAGE, 0)
    for part in range(CHUNKS[TEXT]):
        pass_on(TEXT, part)
    for k in range(1, chips):
        for part in range(CHUNKS[TEXT]):
            arrival(TEXT, part, 2 * k + 1).wait_recv()
        total[IMAGE] += row_pair(k, False)

    def exchange(stage, buffer, count, target, axis):
        copies = []
        for step in range(1, count):
            copies.append(pltpu.make_async_remote_copy(
                src_ref=buffer.at[0],
                dst_ref=buffer.at[step],
                send_sem=sum_send.at[stage, step],
                recv_sem=sum_recv.at[stage, step],
                device_id={axis: target(step)},
                device_id_type=pl.DeviceIdType.MESH,
            ))
            copies[-1].start()
        return copies

    dp_sums[0] = jnp.concatenate(
        [jnp.sum(s, axis=0, keepdims=True) for s in sums] + [jnp.zeros((5, 128), jnp.float32)], axis=0
    )
    dp_copies = exchange(0, dp_sums, n_dp, peer_dp, "dp")

    leave(images_out)
    images_out = send(IMAGE, 1)
    image_grad_ref[...] = unit_pull(own[IMAGE], norms[IMAGE], total[IMAGE], temper)

    pass_on(IMAGE, 0)
    for c in dp_copies:
        c.wait_recv()
    loop_sums[0] = jnp.sum(dp_sums[...], axis=0)
    loop_copies = exchange(1, loop_sums, n_loop, peer_loop, "loop")
    for part in range(CHUNKS[IMAGE] - 1):
        for k in range(1, chips):
            arrival(IMAGE, part, 2 * k + 1).wait_recv()
            total[TEXT] += col_part(image_pair(k, part), False)
        pass_on(IMAGE, part + 1)
    last = CHUNKS[IMAGE] - 1
    for k in range(1, chips):
        total[TEXT] += col_part(units[IMAGE, 2 * k, piece(IMAGE, last)], False)
    for k in range(1, chips):
        arrival(IMAGE, last, 2 * k + 1).wait_recv()
        total[TEXT] += col_part(units[IMAGE, 2 * k + 1, piece(IMAGE, last)], False)
    text_grad_ref[...] = unit_pull(own[TEXT], norms[TEXT], total[TEXT], temper)

    for c in loop_copies:
        c.wait_recv()
    sums_ref[...] = jnp.sum(loop_sums[...], axis=0)

    leave(sent + images_out + dp_copies + loop_copies)


def finish(
    inverse_batch, image_grad, text_grad, sums_ref,
    loss_ref, image_grad_hbm, text_grad_hbm, scale_grad_ref, bias_grad_ref, sems,
):
    stores = [
        pltpu.make_async_copy(image_grad, image_grad_hbm, sems.at[0]),
        pltpu.make_async_copy(text_grad, text_grad_hbm, sems.at[1]),
    ]
    for store in stores:
        store.start()
    loss_ref[0] = jnp.sum(sums_ref[0:1, :]) * inverse_batch
    scale_grad_ref[0] = jnp.sum(sums_ref[1:2, :])
    bias_grad_ref[0] = jnp.sum(sums_ref[2:3, :])
    for store in stores:
        store.wait()


def solution(mesh):
    n_dp, n_loop = mesh.shape["dp"], mesh.shape["loop"]

    def on_device(image_embeds, text_embeds, log_scale, logit_bias):
        rows, width = image_embeds.shape
        scalar = jax.ShapeDtypeStruct((1,), jnp.float32)
        grad = jax.ShapeDtypeStruct((rows, width), jnp.bfloat16)
        hbm = pl.BlockSpec(memory_space=pltpu.HBM)
        vmem = pl.BlockSpec(memory_space=pltpu.VMEM)
        smem = pl.BlockSpec(memory_space=pltpu.SMEM)
        parts = max(CHUNKS)
        image_grad, text_grad, sums = pl.pallas_call(
            functools.partial(kernel, n_dp, n_loop),
            out_shape=(
                pltpu.VMEM((rows, width), jnp.bfloat16),
                pltpu.VMEM((rows, width), jnp.bfloat16),
                pltpu.VMEM((8, 128), jnp.float32),
            ),
            in_specs=[hbm, hbm, smem, smem],
            out_specs=(vmem, vmem, vmem),
            scratch_shapes=[
                pltpu.VMEM((2, rows, width), jnp.bfloat16),
                pltpu.VMEM((2, n_dp, rows, width), jnp.bfloat16),
                pltpu.VMEM((2, rows, width), jnp.float32),
                pltpu.VMEM((2, rows, 1), jnp.float32),
                pltpu.VMEM((n_dp, 8, 128), jnp.float32),
                pltpu.VMEM((n_loop, 8, 128), jnp.float32),
                pltpu.SemaphoreType.DMA((2,)),
                pltpu.SemaphoreType.DMA((2, n_dp, parts)),
                pltpu.SemaphoreType.DMA((2, n_dp, parts)),
                pltpu.SemaphoreType.DMA((2, n_dp, parts)),
                pltpu.SemaphoreType.DMA((2, max(n_dp, n_loop))),
                pltpu.SemaphoreType.DMA((2, max(n_dp, n_loop))),
            ],
            compiler_params=pltpu.CompilerParams(
                collective_id=0, has_side_effects=True, vmem_limit_bytes=32 * 1024 * 1024
            ),
        )(
            pltpu.with_memory_space_constraint(image_embeds, pltpu.HBM),
            pltpu.with_memory_space_constraint(text_embeds, pltpu.HBM),
            log_scale,
            logit_bias,
        )
        return pl.pallas_call(
            functools.partial(finish, 1.0 / (rows * n_dp * n_loop)),
            out_shape=(scalar, grad, grad, scalar, scalar),
            in_specs=[vmem] * 3,
            out_specs=(smem, hbm, hbm, smem, smem),
            scratch_shapes=[pltpu.SemaphoreType.DMA((2,))],
            compiler_params=pltpu.CompilerParams(vmem_limit_bytes=4 * 1024 * 1024),
        )(image_grad, text_grad, sums)

    return jax.shard_map(
        on_device,
        mesh=mesh,
        in_specs=(P(("dp", "loop"), None), P(("dp", "loop"), None), P(), P()),
        out_specs=(P(), P(("dp", "loop"), None), P(("dp", "loop"), None), P(), P()),
        check_vma=False,
    )
```

```python
import functools

import jax
import jax.numpy as jnp
from jax import lax
from jax.experimental import pallas as pl
from jax.experimental.pallas import tpu as pltpu
from jax.sharding import PartitionSpec as P

EPSILON = 1e-06
TEXT, IMAGE = 0, 1
CUTS = ((0, 4, 8), (0, 5, 8))
CHUNKS = tuple(len(cuts) - 1 for cuts in CUTS)


def inverse_norm(floats):
    return lax.rsqrt(jnp.sum(floats * floats, axis=1, keepdims=True) + EPSILON)


def softplus_and_sigmoid(logits):
    small = jnp.exp(-jnp.abs(logits))
    softplus = jnp.maximum(logits, 0.0) + jnp.log1p(small)
    sigmoid = jnp.where(logits >= 0.0, 1.0, small) / (1.0 + small)
    return softplus, sigmoid


def dot_nt(left, right):
    return lax.dot_general(
        left, right, (((1,), (1,)), ((), ())), preferred_element_type=jnp.float32
    )


def unit_pull(embeds, r, cot, temper):
    floats = embeds.astype(jnp.float32)
    along = jnp.sum(floats * cot, axis=1, keepdims=True)
    return ((temper * r) * (cot - floats * (r * r * along))).astype(jnp.bfloat16)


def kernel(
    n_dp, n_loop,
    image_hbm, text_hbm, scale_ref, bias_ref,
    image_grad_ref, text_grad_ref, sums_ref,
    own, units, total, norms, dp_sums, loop_sums,
    load_sem, send_sem, recv_sem, pass_sem, sum_send, sum_recv,
):
    rows = own.shape[1]
    chips = n_dp // 2
    dp, loop = lax.axis_index("dp"), lax.axis_index("loop")
    core = lax.rem(dp, 2)
    sibling = dp + 1 - 2 * core

    def peer_dp(step):
        return lax.rem(dp + step, n_dp)

    def peer_loop(step):
        return lax.rem(loop + step, n_loop)

    def piece(kind, part):
        first, last = CUTS[kind][part] * rows // 8, CUTS[kind][part + 1] * rows // 8
        return pl.ds(first, last - first)

    loads = [
        [
            pltpu.make_async_copy(
                source.at[piece(kind, part)], own.at[kind, piece(kind, part)], load_sem.at[kind, part]
            )
            for part in range(CHUNKS[kind])
        ]
        for kind, source in ((TEXT, text_hbm), (IMAGE, image_hbm))
    ]
    for kind in (TEXT, IMAGE):
        for load in loads[kind]:
            load.start()

    barrier = pltpu.get_barrier_semaphore()
    for step in range(1, n_dp):
        pl.semaphore_signal(barrier, inc=1, device_id={"dp": peer_dp(step)}, device_id_type=pl.DeviceIdType.MESH)
    for step in range(1, n_loop):
        pl.semaphore_signal(barrier, inc=1, device_id={"loop": peer_loop(step)}, device_id_type=pl.DeviceIdType.MESH)

    def normalize(kind, part):
        loads[kind][part].wait()
        floats = own[kind, piece(kind, part)].astype(jnp.float32)
        r = inverse_norm(floats)
        units[kind, 0, piece(kind, part)] = (floats * r).astype(jnp.bfloat16)
        norms[kind, piece(kind, part)] = r

    def copy(kind, part, from_slot, to_slot, target, sem):
        return pltpu.make_async_remote_copy(
            src_ref=units.at[kind, from_slot, piece(kind, part)],
            dst_ref=units.at[kind, to_slot, piece(kind, part)],
            send_sem=sem.at[kind, to_slot, part],
            recv_sem=recv_sem.at[kind, to_slot, part],
            device_id={"dp": target},
            device_id_type=pl.DeviceIdType.MESH,
        )

    sent = []

    def send(kind, part):
        copies = [copy(kind, part, 0, 2 * k, peer_dp(2 * k), send_sem) for k in range(1, chips)]
        for c in copies:
            c.start()
        return copies

    def send_sibling(kind):
        for part in range(CHUNKS[kind]):
            sent.append(copy(kind, part, 0, 1, sibling, send_sem))
            sent[-1].start()

    def leave(copies):
        for c in copies:
            c.wait_send()

    def arrival(kind, part, slot):
        return copy(kind, part, 0, slot, sibling, send_sem)

    def pass_on(kind, part):
        for k in range(1, chips):
            arrival(kind, part, 2 * k).wait_recv()
            sent.append(copy(kind, part, 2 * k, 2 * k + 1, sibling, pass_sem))
            sent[-1].start()

    texts_out = []
    for part in range(CHUNKS[TEXT]):
        normalize(TEXT, part)
        if part == 0:
            pl.semaphore_wait(barrier, n_dp + n_loop - 2)
        texts_out += send(TEXT, part)
    send_sibling(TEXT)
    for part in range(CHUNKS[IMAGE]):
        normalize(IMAGE, part)
    send_sibling(IMAGE)

    temper = jnp.exp(jnp.full((1, 128), scale_ref[0], jnp.float32))[:, :1]
    offset = bias_ref[0]
    image_unit = units[IMAGE, 0]
    text_unit = units[TEXT, 0]

    def eye():
        ids = lax.broadcasted_iota(jnp.int32, (rows, rows), 0)
        return ids == lax.broadcasted_iota(jnp.int32, (rows, rows), 1)

    sums = [jnp.zeros((rows, 128), jnp.float32) for _ in range(3)]

    def folded(values):
        return sum(values[:, c:c + 128] for c in range(0, values.shape[1], 128))

    def less_eye(values, subtrahend):
        wide = jnp.concatenate([eye(), jnp.zeros((rows, rows), jnp.bool_)], axis=1)
        return jnp.where(wide, values - subtrahend, values)

    def row_pair(k, first):
        texts = units[TEXT, 2 * k:2 * k + 2].reshape(2 * rows, -1)
        scaled = temper * dot_nt(image_unit, texts)
        logits = scaled + offset
        losses, coef = softplus_and_sigmoid(logits)
        if first:
            losses = less_eye(losses, logits)
            coef = less_eye(coef, 1.0)
        for i, values in enumerate((losses, coef * scaled, coef)):
            sums[i] += folded(values)
        return jnp.dot(coef.astype(jnp.bfloat16), texts, preferred_element_type=jnp.float32)

    def col_part(images, first):
        logits = temper * dot_nt(text_unit, images) + offset
        _, coef = softplus_and_sigmoid(logits)
        if first:
            coef = less_eye(coef, 1.0)
        return jnp.dot(coef.astype(jnp.bfloat16), images, preferred_element_type=jnp.float32)

    def image_pair(k, part):
        return units[IMAGE, 2 * k:2 * k + 2, piece(IMAGE, part)].reshape(-1, units.shape[3])

    for part in range(CHUNKS[TEXT]):
        arrival(TEXT, part, 1).wait_recv()
    total[IMAGE] = row_pair(0, True)
    for part in range(CHUNKS[IMAGE]):
        arrival(IMAGE, part, 1).wait_recv()
    total[TEXT] = col_part(units[IMAGE, 0:2].reshape(2 * rows, -1), True)
    leave(texts_out)
    images_out = send(IMAGE, 0)
    for part in range(CHUNKS[TEXT]):
        pass_on(TEXT, part)
    for k in range(1, chips):
        for part in range(CHUNKS[TEXT]):
            arrival(TEXT, part, 2 * k + 1).wait_recv()
        total[IMAGE] += row_pair(k, False)

    def exchange(stage, buffer, count, target, axis):
        copies = []
        for step in range(1, count):
            copies.append(pltpu.make_async_remote_copy(
                src_ref=buffer.at[0],
                dst_ref=buffer.at[step],
                send_sem=sum_send.at[stage, step],
                recv_sem=sum_recv.at[stage, step],
                device_id={axis: target(step)},
                device_id_type=pl.DeviceIdType.MESH,
            ))
            copies[-1].start()
        return copies

    dp_sums[0] = jnp.concatenate(
        [jnp.sum(s, axis=0, keepdims=True) for s in sums] + [jnp.zeros((5, 128), jnp.float32)], axis=0
    )
    dp_copies = exchange(0, dp_sums, n_dp, peer_dp, "dp")

    leave(images_out)
    images_out = send(IMAGE, 1)
    image_grad_ref[...] = unit_pull(own[IMAGE], norms[IMAGE], total[IMAGE], temper)

    pass_on(IMAGE, 0)
    for c in dp_copies:
        c.wait_recv()
    loop_sums[0] = jnp.sum(dp_sums[...], axis=0)
    loop_copies = exchange(1, loop_sums, n_loop, peer_loop, "loop")
    for part in range(CHUNKS[IMAGE] - 1):
        for k in range(1, chips):
            arrival(IMAGE, part, 2 * k + 1).wait_recv()
            total[TEXT] += col_part(image_pair(k, part), False)
        pass_on(IMAGE, part + 1)
    last = CHUNKS[IMAGE] - 1
    for k in range(1, chips):
        total[TEXT] += col_part(units[IMAGE, 2 * k, piece(IMAGE, last)], False)
    for k in range(1, chips):
        arrival(IMAGE, last, 2 * k + 1).wait_recv()
        total[TEXT] += col_part(units[IMAGE, 2 * k + 1, piece(IMAGE, last)], False)
    text_grad_ref[...] = unit_pull(own[TEXT], norms[TEXT], total[TEXT], temper)

    for c in loop_copies:
        c.wait_recv()
    sums_ref[...] = jnp.sum(loop_sums[...], axis=0)

    leave(sent + images_out + dp_copies + loop_copies)


def finish(
    inverse_batch, image_grad, text_grad, sums_ref,
    loss_hbm, image_grad_hbm, text_grad_hbm, scale_grad_hbm, bias_grad_hbm, scalars, sems,
):
    stores = [
        pltpu.make_async_copy(image_grad, image_grad_hbm, sems.at[0]),
        pltpu.make_async_copy(text_grad, text_grad_hbm, sems.at[1]),
    ]
    for store in stores:
        store.start()
    totals = jnp.sum(sums_ref[...], axis=1, keepdims=True)
    for i, (target, factor) in enumerate(((loss_hbm, inverse_batch), (scale_grad_hbm, 1.0), (bias_grad_hbm, 1.0))):
        scalars[i, 0] = totals[i, 0] * factor
        stores.append(pltpu.make_async_copy(scalars.at[i], target, sems.at[2 + i]))
        stores[-1].start()
    for store in stores:
        store.wait()


def solution(mesh):
    n_dp, n_loop = mesh.shape["dp"], mesh.shape["loop"]

    def on_device(image_embeds, text_embeds, log_scale, logit_bias):
        rows, width = image_embeds.shape
        scalar = jax.ShapeDtypeStruct((1,), jnp.float32)
        grad = jax.ShapeDtypeStruct((rows, width), jnp.bfloat16)
        hbm = pl.BlockSpec(memory_space=pltpu.HBM)
        vmem = pl.BlockSpec(memory_space=pltpu.VMEM)
        smem = pl.BlockSpec(memory_space=pltpu.SMEM)
        parts = max(CHUNKS)
        image_grad, text_grad, sums = pl.pallas_call(
            functools.partial(kernel, n_dp, n_loop),
            out_shape=(
                pltpu.VMEM((rows, width), jnp.bfloat16),
                pltpu.VMEM((rows, width), jnp.bfloat16),
                pltpu.VMEM((8, 128), jnp.float32),
            ),
            in_specs=[hbm, hbm, smem, smem],
            out_specs=(vmem, vmem, vmem),
            scratch_shapes=[
                pltpu.VMEM((2, rows, width), jnp.bfloat16),
                pltpu.VMEM((2, n_dp, rows, width), jnp.bfloat16),
                pltpu.VMEM((2, rows, width), jnp.float32),
                pltpu.VMEM((2, rows, 1), jnp.float32),
                pltpu.VMEM((n_dp, 8, 128), jnp.float32),
                pltpu.VMEM((n_loop, 8, 128), jnp.float32),
                pltpu.SemaphoreType.DMA((2, parts)),
                pltpu.SemaphoreType.DMA((2, n_dp, parts)),
                pltpu.SemaphoreType.DMA((2, n_dp, parts)),
                pltpu.SemaphoreType.DMA((2, n_dp, parts)),
                pltpu.SemaphoreType.DMA((2, max(n_dp, n_loop))),
                pltpu.SemaphoreType.DMA((2, max(n_dp, n_loop))),
            ],
            compiler_params=pltpu.CompilerParams(
                collective_id=0, has_side_effects=True, vmem_limit_bytes=32 * 1024 * 1024
            ),
        )(
            pltpu.with_memory_space_constraint(image_embeds, pltpu.HBM),
            pltpu.with_memory_space_constraint(text_embeds, pltpu.HBM),
            log_scale,
            logit_bias,
        )
        return pl.pallas_call(
            functools.partial(finish, 1.0 / (rows * n_dp * n_loop)),
            out_shape=(scalar, grad, grad, scalar, scalar),
            in_specs=[vmem] * 3,
            out_specs=(hbm, hbm, hbm, hbm, hbm),
            scratch_shapes=[pltpu.SMEM((3, 1), jnp.float32), pltpu.SemaphoreType.DMA((5,))],
            compiler_params=pltpu.CompilerParams(vmem_limit_bytes=4 * 1024 * 1024),
        )(image_grad, text_grad, sums)

    return jax.shard_map(
        on_device,
        mesh=mesh,
        in_specs=(P(("dp", "loop"), None), P(("dp", "loop"), None), P(), P()),
        out_specs=(P(), P(("dp", "loop"), None), P(("dp", "loop"), None), P(), P()),
        check_vma=False,
    )
```

```python
import functools

import jax
import jax.numpy as jnp
from jax import lax
from jax.experimental import pallas as pl
from jax.experimental.pallas import tpu as pltpu
from jax.sharding import PartitionSpec as P

EPSILON = 1e-06
TEXT, IMAGE = 0, 1
CUTS = ((0, 4, 8), (0, 5, 8))
CHUNKS = tuple(len(cuts) - 1 for cuts in CUTS)


def inverse_norm(floats):
    return lax.rsqrt(jnp.sum(floats * floats, axis=1, keepdims=True) + EPSILON)


def softplus_and_sigmoid(logits):
    small = jnp.exp(-jnp.abs(logits))
    softplus = jnp.maximum(logits, 0.0) + jnp.log1p(small)
    sigmoid = jnp.where(logits >= 0.0, 1.0, small) / (1.0 + small)
    return softplus, sigmoid


def dot_nt(left, right):
    return lax.dot_general(
        left, right, (((1,), (1,)), ((), ())), preferred_element_type=jnp.float32
    )


def unit_pull(embeds, r, cot, temper):
    floats = embeds.astype(jnp.float32)
    along = jnp.sum(floats * cot, axis=1, keepdims=True)
    return ((temper * r) * (cot - floats * (r * r * along))).astype(jnp.bfloat16)


def kernel(
    n_dp, n_loop,
    image_hbm, text_hbm, scale_ref, bias_ref,
    image_grad_ref, text_grad_ref, sums_ref,
    own, units, total, norms, dp_sums, loop_sums,
    load_sem, send_sem, recv_sem, pass_sem, sum_send, sum_recv,
):
    rows = own.shape[1]
    chips = n_dp // 2
    dp, loop = lax.axis_index("dp"), lax.axis_index("loop")
    core = lax.rem(dp, 2)
    sibling = dp + 1 - 2 * core

    def peer_dp(step):
        return lax.rem(dp + step, n_dp)

    def peer_loop(step):
        return lax.rem(loop + step, n_loop)

    def piece(kind, part):
        first, last = CUTS[kind][part] * rows // 8, CUTS[kind][part + 1] * rows // 8
        return pl.ds(first, last - first)

    barrier = pltpu.get_barrier_semaphore()
    for step in range(1, n_dp):
        pl.semaphore_signal(barrier, inc=1, device_id={"dp": peer_dp(step)}, device_id_type=pl.DeviceIdType.MESH)
    for step in range(1, n_loop):
        pl.semaphore_signal(barrier, inc=1, device_id={"loop": peer_loop(step)}, device_id_type=pl.DeviceIdType.MESH)

    loads = [
        [
            pltpu.make_async_copy(
                source.at[piece(kind, part)], own.at[kind, piece(kind, part)], load_sem.at[kind, part]
            )
            for part in range(CHUNKS[kind])
        ]
        for kind, source in ((TEXT, text_hbm), (IMAGE, image_hbm))
    ]
    for kind in (TEXT, IMAGE):
        for load in loads[kind]:
            load.start()

    def normalize(kind, part):
        loads[kind][part].wait()
        floats = own[kind, piece(kind, part)].astype(jnp.float32)
        r = inverse_norm(floats)
        units[kind, 0, piece(kind, part)] = (floats * r).astype(jnp.bfloat16)
        norms[kind, piece(kind, part)] = r

    def copy(kind, part, from_slot, to_slot, target, sem):
        return pltpu.make_async_remote_copy(
            src_ref=units.at[kind, from_slot, piece(kind, part)],
            dst_ref=units.at[kind, to_slot, piece(kind, part)],
            send_sem=sem.at[kind, to_slot, part],
            recv_sem=recv_sem.at[kind, to_slot, part],
            device_id={"dp": target},
            device_id_type=pl.DeviceIdType.MESH,
        )

    sent = []

    def send(kind, part):
        copies = [copy(kind, part, 0, 2 * k, peer_dp(2 * k), send_sem) for k in range(1, chips)]
        for c in copies:
            c.start()
        return copies

    def send_sibling(kind):
        for part in range(CHUNKS[kind]):
            sent.append(copy(kind, part, 0, 1, sibling, send_sem))
            sent[-1].start()

    def leave(copies):
        for c in copies:
            c.wait_send()

    def arrival(kind, part, slot):
        return copy(kind, part, 0, slot, sibling, send_sem)

    def pass_on(kind, part):
        for k in range(1, chips):
            arrival(kind, part, 2 * k).wait_recv()
            sent.append(copy(kind, part, 2 * k, 2 * k + 1, sibling, pass_sem))
            sent[-1].start()

    texts_out = []
    for part in range(CHUNKS[TEXT]):
        normalize(TEXT, part)
        if part == 0:
            pl.semaphore_wait(barrier, n_dp + n_loop - 2)
        texts_out += send(TEXT, part)
    send_sibling(TEXT)
    for part in range(CHUNKS[IMAGE]):
        normalize(IMAGE, part)
    send_sibling(IMAGE)

    temper = jnp.exp(jnp.full((1, 128), scale_ref[0], jnp.float32))[:, :1]
    offset = bias_ref[0]
    image_unit = units[IMAGE, 0]
    text_unit = units[TEXT, 0]

    def eye():
        ids = lax.broadcasted_iota(jnp.int32, (rows, rows), 0)
        return ids == lax.broadcasted_iota(jnp.int32, (rows, rows), 1)

    sums = [jnp.zeros((rows, 128), jnp.float32) for _ in range(3)]

    def folded(values):
        return sum(values[:, c:c + 128] for c in range(0, values.shape[1], 128))

    def less_eye(values, subtrahend):
        wide = jnp.concatenate([eye(), jnp.zeros((rows, rows), jnp.bool_)], axis=1)
        return jnp.where(wide, values - subtrahend, values)

    def row_part(texts, first):
        scaled = temper * dot_nt(image_unit, texts)
        logits = scaled + offset
        losses, coef = softplus_and_sigmoid(logits)
        if first:
            losses = less_eye(losses, logits)
            coef = less_eye(coef, 1.0)
        for i, values in enumerate((losses, coef * scaled, coef)):
            sums[i] += folded(values)
        return jnp.dot(coef.astype(jnp.bfloat16), texts, preferred_element_type=jnp.float32)

    def col_part(images, first):
        logits = temper * dot_nt(text_unit, images) + offset
        _, coef = softplus_and_sigmoid(logits)
        if first:
            coef = less_eye(coef, 1.0)
        return jnp.dot(coef.astype(jnp.bfloat16), images, preferred_element_type=jnp.float32)

    for part in range(CHUNKS[TEXT]):
        arrival(TEXT, part, 1).wait_recv()
    total[IMAGE] = row_part(units[TEXT, 0:2].reshape(2 * rows, -1), True)
    for part in range(CHUNKS[IMAGE]):
        arrival(IMAGE, part, 1).wait_recv()
    total[TEXT] = col_part(units[IMAGE, 0:2].reshape(2 * rows, -1), True)
    leave(texts_out)
    images_out = send(IMAGE, 0)
    for part in range(CHUNKS[TEXT]):
        pass_on(TEXT, part)
    for k in range(1, chips):
        total[IMAGE] += row_part(units[TEXT, 2 * k], False)
    for k in range(1, chips):
        for part in range(CHUNKS[TEXT]):
            arrival(TEXT, part, 2 * k + 1).wait_recv()
        total[IMAGE] += row_part(units[TEXT, 2 * k + 1], False)
    leave(images_out)
    images_out = send(IMAGE, 1)

    def exchange(stage, buffer, count, target, axis):
        copies = []
        for step in range(1, count):
            copies.append(pltpu.make_async_remote_copy(
                src_ref=buffer.at[0],
                dst_ref=buffer.at[step],
                send_sem=sum_send.at[stage, step],
                recv_sem=sum_recv.at[stage, step],
                device_id={axis: target(step)},
                device_id_type=pl.DeviceIdType.MESH,
            ))
            copies[-1].start()
        return copies

    dp_sums[0] = jnp.concatenate(
        [jnp.sum(s, axis=0, keepdims=True) for s in sums] + [jnp.zeros((5, 128), jnp.float32)], axis=0
    )
    dp_copies = exchange(0, dp_sums, n_dp, peer_dp, "dp")

    image_grad_ref[...] = unit_pull(own[IMAGE], norms[IMAGE], total[IMAGE], temper)

    pass_on(IMAGE, 0)
    for c in dp_copies:
        c.wait_recv()
    loop_sums[0] = jnp.sum(dp_sums[...], axis=0)
    loop_copies = exchange(1, loop_sums, n_loop, peer_loop, "loop")
    for part in range(CHUNKS[IMAGE]):
        if part:
            pass_on(IMAGE, part)
        for k in range(1, chips):
            total[TEXT] += col_part(units[IMAGE, 2 * k, piece(IMAGE, part)], False)
        for k in range(1, chips):
            arrival(IMAGE, part, 2 * k + 1).wait_recv()
            total[TEXT] += col_part(units[IMAGE, 2 * k + 1, piece(IMAGE, part)], False)
    text_grad_ref[...] = unit_pull(own[TEXT], norms[TEXT], total[TEXT], temper)

    for c in loop_copies:
        c.wait_recv()
    sums_ref[...] = jnp.sum(loop_sums[...], axis=0)

    leave(sent + images_out + dp_copies + loop_copies)


def finish(
    inverse_batch, image_grad, text_grad, sums_ref,
    loss_hbm, image_grad_hbm, text_grad_hbm, scale_grad_hbm, bias_grad_hbm, scalars, sems,
):
    stores = [
        pltpu.make_async_copy(image_grad, image_grad_hbm, sems.at[0]),
        pltpu.make_async_copy(text_grad, text_grad_hbm, sems.at[1]),
    ]
    for store in stores:
        store.start()
    totals = jnp.sum(sums_ref[...], axis=1, keepdims=True)
    for i, (target, factor) in enumerate(((loss_hbm, inverse_batch), (scale_grad_hbm, 1.0), (bias_grad_hbm, 1.0))):
        scalars[i, 0] = totals[i, 0] * factor
        stores.append(pltpu.make_async_copy(scalars.at[i], target, sems.at[2 + i]))
        stores[-1].start()
    for store in stores:
        store.wait()


def solution(mesh):
    n_dp, n_loop = mesh.shape["dp"], mesh.shape["loop"]

    def on_device(image_embeds, text_embeds, log_scale, logit_bias):
        rows, width = image_embeds.shape
        scalar = jax.ShapeDtypeStruct((1,), jnp.float32)
        grad = jax.ShapeDtypeStruct((rows, width), jnp.bfloat16)
        hbm = pl.BlockSpec(memory_space=pltpu.HBM)
        vmem = pl.BlockSpec(memory_space=pltpu.VMEM)
        smem = pl.BlockSpec(memory_space=pltpu.SMEM)
        parts = max(CHUNKS)
        image_grad, text_grad, sums = pl.pallas_call(
            functools.partial(kernel, n_dp, n_loop),
            out_shape=(
                pltpu.VMEM((rows, width), jnp.bfloat16),
                pltpu.VMEM((rows, width), jnp.bfloat16),
                pltpu.VMEM((8, 128), jnp.float32),
            ),
            in_specs=[hbm, hbm, smem, smem],
            out_specs=(vmem, vmem, vmem),
            scratch_shapes=[
                pltpu.VMEM((2, rows, width), jnp.bfloat16),
                pltpu.VMEM((2, n_dp, rows, width), jnp.bfloat16),
                pltpu.VMEM((2, rows, width), jnp.float32),
                pltpu.VMEM((2, rows, 1), jnp.float32),
                pltpu.VMEM((n_dp, 8, 128), jnp.float32),
                pltpu.VMEM((n_loop, 8, 128), jnp.float32),
                pltpu.SemaphoreType.DMA((2, parts)),
                pltpu.SemaphoreType.DMA((2, n_dp, parts)),
                pltpu.SemaphoreType.DMA((2, n_dp, parts)),
                pltpu.SemaphoreType.DMA((2, n_dp, parts)),
                pltpu.SemaphoreType.DMA((2, max(n_dp, n_loop))),
                pltpu.SemaphoreType.DMA((2, max(n_dp, n_loop))),
            ],
            compiler_params=pltpu.CompilerParams(
                collective_id=0, has_side_effects=True, vmem_limit_bytes=32 * 1024 * 1024
            ),
        )(
            pltpu.with_memory_space_constraint(image_embeds, pltpu.HBM),
            pltpu.with_memory_space_constraint(text_embeds, pltpu.HBM),
            log_scale,
            logit_bias,
        )
        return pl.pallas_call(
            functools.partial(finish, 1.0 / (rows * n_dp * n_loop)),
            out_shape=(scalar, grad, grad, scalar, scalar),
            in_specs=[vmem] * 3,
            out_specs=(hbm, hbm, hbm, hbm, hbm),
            scratch_shapes=[pltpu.SMEM((3, 1), jnp.float32), pltpu.SemaphoreType.DMA((5,))],
            compiler_params=pltpu.CompilerParams(vmem_limit_bytes=4 * 1024 * 1024),
        )(image_grad, text_grad, sums)

    return jax.shard_map(
        on_device,
        mesh=mesh,
        in_specs=(P(("dp", "loop"), None), P(("dp", "loop"), None), P(), P()),
        out_specs=(P(), P(("dp", "loop"), None), P(("dp", "loop"), None), P(), P()),
        check_vma=False,
    )
```

```python
import functools

import jax
import jax.numpy as jnp
from jax import lax
from jax.experimental import pallas as pl
from jax.experimental.pallas import tpu as pltpu
from jax.sharding import PartitionSpec as P

EPSILON = 1e-06
TEXT, IMAGE = 0, 1
CUTS = ((0, 4, 8), (0, 5, 8))
CHUNKS = tuple(len(cuts) - 1 for cuts in CUTS)


def inverse_norm(floats):
    return lax.rsqrt(jnp.sum(floats * floats, axis=1, keepdims=True) + EPSILON)


def softplus_and_sigmoid(logits):
    small = jnp.exp(-jnp.abs(logits))
    softplus = jnp.maximum(logits, 0.0) + jnp.log1p(small)
    sigmoid = jnp.where(logits >= 0.0, 1.0, small) / (1.0 + small)
    return softplus, sigmoid


def dot_nt(left, right):
    return lax.dot_general(
        left, right, (((1,), (1,)), ((), ())), preferred_element_type=jnp.float32
    )


def unit_pull(embeds, r, cot, temper):
    floats = embeds.astype(jnp.float32)
    along = jnp.sum(floats * cot, axis=1, keepdims=True)
    return ((temper * r) * (cot - floats * (r * r * along))).astype(jnp.bfloat16)


def kernel(
    n_dp, n_loop,
    image_hbm, text_hbm, scale_ref, bias_ref,
    image_grad_ref, text_grad_ref, sums_ref,
    own, units, total, norms, dp_sums, loop_sums,
    load_sem, send_sem, recv_sem, pass_sem, sum_send, sum_recv,
):
    rows = own.shape[1]
    chips = n_dp // 2
    dp, loop = lax.axis_index("dp"), lax.axis_index("loop")
    core = lax.rem(dp, 2)
    sibling = dp + 1 - 2 * core

    def peer_dp(step):
        return lax.rem(dp + step, n_dp)

    def peer_loop(step):
        return lax.rem(loop + step, n_loop)

    def piece(kind, part):
        first, last = CUTS[kind][part] * rows // 8, CUTS[kind][part + 1] * rows // 8
        return pl.ds(first, last - first)

    loads = [
        [
            pltpu.make_async_copy(
                source.at[piece(kind, part)], own.at[kind, piece(kind, part)], load_sem.at[kind, part]
            )
            for part in range(CHUNKS[kind])
        ]
        for kind, source in ((TEXT, text_hbm), (IMAGE, image_hbm))
    ]
    for kind in (TEXT, IMAGE):
        for load in loads[kind]:
            load.start()

    barrier = pltpu.get_barrier_semaphore()
    for step in range(1, n_dp):
        pl.semaphore_signal(barrier, inc=1, device_id={"dp": peer_dp(step)}, device_id_type=pl.DeviceIdType.MESH)
    for step in range(1, n_loop):
        pl.semaphore_signal(barrier, inc=1, device_id={"loop": peer_loop(step)}, device_id_type=pl.DeviceIdType.MESH)

    def normalize(kind, part):
        loads[kind][part].wait()
        floats = own[kind, piece(kind, part)].astype(jnp.float32)
        r = inverse_norm(floats)
        units[kind, 0, piece(kind, part)] = (floats * r).astype(jnp.bfloat16)
        norms[kind, piece(kind, part)] = r

    def copy(kind, part, from_slot, to_slot, target, sem):
        return pltpu.make_async_remote_copy(
            src_ref=units.at[kind, from_slot, piece(kind, part)],
            dst_ref=units.at[kind, to_slot, piece(kind, part)],
            send_sem=sem.at[kind, to_slot, part],
            recv_sem=recv_sem.at[kind, to_slot, part],
            device_id={"dp": target},
            device_id_type=pl.DeviceIdType.MESH,
        )

    sent = []

    def send(kind, part):
        copies = [copy(kind, part, 0, 2 * k, peer_dp(2 * k), send_sem) for k in range(1, chips)]
        for c in copies:
            c.start()
        return copies

    def send_sibling(kind):
        for part in range(CHUNKS[kind]):
            sent.append(copy(kind, part, 0, 1, sibling, send_sem))
            sent[-1].start()

    def leave(copies):
        for c in copies:
            c.wait_send()

    def arrival(kind, part, slot):
        return copy(kind, part, 0, slot, sibling, send_sem)

    def pass_on(kind, part):
        for k in range(1, chips):
            arrival(kind, part, 2 * k).wait_recv()
            sent.append(copy(kind, part, 2 * k, 2 * k + 1, sibling, pass_sem))
            sent[-1].start()

    texts_out = []
    for part in range(CHUNKS[TEXT]):
        normalize(TEXT, part)
        if part == 0:
            pl.semaphore_wait(barrier, n_dp + n_loop - 2)
        texts_out += send(TEXT, part)
    send_sibling(TEXT)
    for part in range(CHUNKS[IMAGE]):
        normalize(IMAGE, part)
    send_sibling(IMAGE)

    temper = jnp.exp(jnp.full((1, 128), scale_ref[0], jnp.float32))[:, :1]
    offset = bias_ref[0]
    image_unit = units[IMAGE, 0]
    text_unit = units[TEXT, 0]

    def eye():
        ids = lax.broadcasted_iota(jnp.int32, (rows, rows), 0)
        return ids == lax.broadcasted_iota(jnp.int32, (rows, rows), 1)

    sums = [jnp.zeros((rows, 128), jnp.float32) for _ in range(3)]

    def folded(values):
        return sum(values[:, c:c + 128] for c in range(0, values.shape[1], 128))

    def less_eye(values, subtrahend):
        wide = jnp.concatenate([eye(), jnp.zeros((rows, rows), jnp.bool_)], axis=1)
        return jnp.where(wide, values - subtrahend, values)

    def row_pair(k, first):
        texts = units[TEXT, 2 * k:2 * k + 2].reshape(2 * rows, -1)
        scaled = temper * dot_nt(image_unit, texts)
        logits = scaled + offset
        losses, coef = softplus_and_sigmoid(logits)
        if first:
            losses = less_eye(losses, logits)
            coef = less_eye(coef, 1.0)
        for i, values in enumerate((losses, coef * scaled, coef)):
            sums[i] += folded(values)
        return jnp.dot(coef.astype(jnp.bfloat16), texts, preferred_element_type=jnp.float32)

    def col_part(images, first):
        logits = temper * dot_nt(text_unit, images) + offset
        _, coef = softplus_and_sigmoid(logits)
        if first:
            coef = less_eye(coef, 1.0)
        return jnp.dot(coef.astype(jnp.bfloat16), images, preferred_element_type=jnp.float32)

    def image_pair(k, part):
        return units[IMAGE, 2 * k:2 * k + 2, piece(IMAGE, part)].reshape(-1, units.shape[3])

    for part in range(CHUNKS[TEXT]):
        arrival(TEXT, part, 1).wait_recv()
    total[IMAGE] = row_pair(0, True)
    for part in range(CHUNKS[IMAGE]):
        arrival(IMAGE, part, 1).wait_recv()
    total[TEXT] = col_part(units[IMAGE, 0:2].reshape(2 * rows, -1), True)
    leave(texts_out)
    images_out = send(IMAGE, 0)
    for part in range(CHUNKS[TEXT]):
        pass_on(TEXT, part)
    for k in range(1, chips):
        for part in range(CHUNKS[TEXT]):
            arrival(TEXT, part, 2 * k + 1).wait_recv()
        total[IMAGE] += row_pair(k, False)

    def exchange(stage, buffer, count, target, axis):
        copies = []
        for step in range(1, count):
            copies.append(pltpu.make_async_remote_copy(
                src_ref=buffer.at[0],
                dst_ref=buffer.at[step],
                send_sem=sum_send.at[stage, step],
                recv_sem=sum_recv.at[stage, step],
                device_id={axis: target(step)},
                device_id_type=pl.DeviceIdType.MESH,
            ))
            copies[-1].start()
        return copies

    dp_sums[0] = jnp.concatenate(
        [jnp.sum(s, axis=0, keepdims=True) for s in sums] + [jnp.zeros((5, 128), jnp.float32)], axis=0
    )
    dp_copies = exchange(0, dp_sums, n_dp, peer_dp, "dp")

    leave(images_out)
    images_out = send(IMAGE, 1)
    image_grad_ref[...] = unit_pull(own[IMAGE], norms[IMAGE], total[IMAGE], temper)

    pass_on(IMAGE, 0)
    for c in dp_copies:
        c.wait_recv()
    loop_sums[0] = jnp.sum(dp_sums[...], axis=0)
    loop_copies = exchange(1, loop_sums, n_loop, peer_loop, "loop")
    for part in range(CHUNKS[IMAGE]):
        if part:
            pass_on(IMAGE, part)
        for k in range(1, chips):
            arrival(IMAGE, part, 2 * k + 1).wait_recv()
            total[TEXT] += col_part(image_pair(k, part), False)
    text_grad_ref[...] = unit_pull(own[TEXT], norms[TEXT], total[TEXT], temper)

    for c in loop_copies:
        c.wait_recv()
    sums_ref[...] = jnp.sum(loop_sums[...], axis=0)

    leave(sent + images_out + dp_copies + loop_copies)


def finish(
    inverse_batch, image_grad, text_grad, sums_ref,
    loss_hbm, image_grad_hbm, text_grad_hbm, scale_grad_hbm, bias_grad_hbm, scalars, sems,
):
    stores = [
        pltpu.make_async_copy(image_grad, image_grad_hbm, sems.at[0]),
        pltpu.make_async_copy(text_grad, text_grad_hbm, sems.at[1]),
    ]
    for store in stores:
        store.start()
    totals = jnp.sum(sums_ref[...], axis=1, keepdims=True)
    for i, (target, factor) in enumerate(((loss_hbm, inverse_batch), (scale_grad_hbm, 1.0), (bias_grad_hbm, 1.0))):
        scalars[i, 0] = totals[i, 0] * factor
        stores.append(pltpu.make_async_copy(scalars.at[i], target, sems.at[2 + i]))
        stores[-1].start()
    for store in stores:
        store.wait()


def solution(mesh):
    n_dp, n_loop = mesh.shape["dp"], mesh.shape["loop"]

    def on_device(image_embeds, text_embeds, log_scale, logit_bias):
        rows, width = image_embeds.shape
        scalar = jax.ShapeDtypeStruct((1,), jnp.float32)
        grad = jax.ShapeDtypeStruct((rows, width), jnp.bfloat16)
        hbm = pl.BlockSpec(memory_space=pltpu.HBM)
        vmem = pl.BlockSpec(memory_space=pltpu.VMEM)
        smem = pl.BlockSpec(memory_space=pltpu.SMEM)
        parts = max(CHUNKS)
        image_grad, text_grad, sums = pl.pallas_call(
            functools.partial(kernel, n_dp, n_loop),
            out_shape=(
                pltpu.VMEM((rows, width), jnp.bfloat16),
                pltpu.VMEM((rows, width), jnp.bfloat16),
                pltpu.VMEM((8, 128), jnp.float32),
            ),
            in_specs=[hbm, hbm, smem, smem],
            out_specs=(vmem, vmem, vmem),
            scratch_shapes=[
                pltpu.VMEM((2, rows, width), jnp.bfloat16),
                pltpu.VMEM((2, n_dp, rows, width), jnp.bfloat16),
                pltpu.VMEM((2, rows, width), jnp.float32),
                pltpu.VMEM((2, rows, 1), jnp.float32),
                pltpu.VMEM((n_dp, 8, 128), jnp.float32),
                pltpu.VMEM((n_loop, 8, 128), jnp.float32),
                pltpu.SemaphoreType.DMA((2, parts)),
                pltpu.SemaphoreType.DMA((2, n_dp, parts)),
                pltpu.SemaphoreType.DMA((2, n_dp, parts)),
                pltpu.SemaphoreType.DMA((2, n_dp, parts)),
                pltpu.SemaphoreType.DMA((2, max(n_dp, n_loop))),
                pltpu.SemaphoreType.DMA((2, max(n_dp, n_loop))),
            ],
            compiler_params=pltpu.CompilerParams(
                collective_id=0, has_side_effects=True, vmem_limit_bytes=32 * 1024 * 1024
            ),
        )(
            pltpu.with_memory_space_constraint(image_embeds, pltpu.HBM),
            pltpu.with_memory_space_constraint(text_embeds, pltpu.HBM),
            log_scale,
            logit_bias,
        )
        return pl.pallas_call(
            functools.partial(finish, 1.0 / (rows * n_dp * n_loop)),
            out_shape=(scalar, grad, grad, scalar, scalar),
            in_specs=[vmem] * 3,
            out_specs=(hbm, hbm, hbm, hbm, hbm),
            scratch_shapes=[pltpu.SMEM((3, 1), jnp.float32), pltpu.SemaphoreType.DMA((5,))],
            compiler_params=pltpu.CompilerParams(vmem_limit_bytes=4 * 1024 * 1024),
        )(image_grad, text_grad, sums)

    return jax.shard_map(
        on_device,
        mesh=mesh,
        in_specs=(P(("dp", "loop"), None), P(("dp", "loop"), None), P(), P()),
        out_specs=(P(), P(("dp", "loop"), None), P(("dp", "loop"), None), P(), P()),
        check_vma=False,
    )
```
